128 devices in a mesh: section: 2 (over x_hi), dp: 16 (over x_lo, y, core), node: 4 (over z).
Axes of the slice: x: 4 (x_hi: 2, x_lo: 2; x = x_hi * 2 + x_lo), y: 4, z: 4, core: 2. Of those that a mesh axis runs over, the one named last changes fastest.
Arguments:
- hidden_in: bfloat16 [2, 16384, 8192], P('section', ('dp', 'node')), may hold values from -8 to 8
- norm_gain: float32 [2, 8192], P('section'), may hold values from 0.1 to 1.9
- weight_codes: int32 [2, 8192, 1024], P('section', 'node'), may hold values from -127 to 127
- block_scales: float32 [2, 32, 1024], P('section', 'node'), may hold values from 7e-05 to 0.0003
- value_grad: bfloat16 [2, 16384, 1024], P('section', ('dp', 'node')), may hold values from -16 to 16
Outputs:
- passed_values: bfloat16 [2, 16384, 1024], P('section', ('dp', 'node'))
- input_grad: bfloat16 [2, 16384, 8192], P('section', ('dp', 'node'))
- weight_grad: bfloat16 [2, 8192, 1024], P('section', ('dp', 'node'))
The draws below stay inside these ranges and needn't reach their ends.
All inputs are finite; a program needn't handle non-finite values.
Results may differ from the reference program's by a relative error of at most 0.025.
Values may be sent and summed in bfloat16 or wider, within the bound.
A program may use at most 192 MiB of HBM per device.

```python
import math
import jax
import jax.numpy as jnp
from jax import lax

D = 8192
KV = 1024
BLOCK = 256
TOK_DEV = 256
TOKENS = 16384
SECTIONS = 2
N_DP = 16
N_NODE = 4


def touch_ends(result, rng, smallest, high):
    spot = [jax.random.randint(jax.random.fold_in(rng, axis), (), 0, length) for axis, length in enumerate(result.shape)]
    widest = result.shape.index(max(result.shape))
    beside = spot[:widest] + [(spot[widest] + 1) % result.shape[widest]] + spot[widest + 1:]
    return result.at[tuple(spot)].set(smallest).at[tuple(beside)].set(high)


def with_spikes(array, rng, source, target, parts, factor):
    def block_of(position):
        return (jnp.arange(array.shape[position]) // (array.shape[position] // parts)).reshape((-1,) + (1,) * (array.ndim - 1 - position))

    one_side = jax.random.permutation(rng, parts)[block_of(target)]
    other_side = (block_of(target) + parts // 2) % parts
    return jnp.where((block_of(source) == one_side) | (block_of(source) == other_side), factor * array, array)


def shard_levels(stream_key, shape, cuts, least, high):
    def one(dim, parts):
        heights = jax.random.uniform(jax.random.fold_in(jax.random.fold_in(stream_key, 6), dim), (parts,), jnp.float32, least / len(cuts), high / len(cuts))
        return jnp.repeat(jnp.exp(heights), shape[dim] // parts).reshape((-1,) + (1,) * (len(shape) - dim - 1))

    loudness = one(*cuts[0])
    for cut in cuts[1:]:
        loudness = loudness * one(*cut)
    return loudness


def bell_draw(key, shape, deviation, most, split=(), kind=jnp.bfloat16):
    factor_of = shard_levels(key, shape, split, -0.22, 0.18) if split else 1.0
    values = jax.random.normal(key, shape, jnp.float32) * deviation * factor_of
    return jnp.minimum(jnp.maximum(values, -most), most).astype(kind)


def heavy_noise(stream_key, shape, deviation, reach, split, heavy, kind=jnp.bfloat16):
    values = deviation * jax.random.normal(stream_key, shape, jnp.float32)
    if split:
        values = values * shard_levels(stream_key, shape, split, -0.22, 0.18)
    return jnp.clip(with_spikes(values, jax.random.fold_in(stream_key, 3), *heavy), -reach, reach).astype(kind)


def setup_inputs(seed: int = 0) -> dict:
    splits = jax.random.split(jax.random.key(seed), 6)
    return {
        "hidden_in": heavy_noise(splits[0], (SECTIONS, TOKENS, D), 1.0, 8.0, ((0, 2), (1, 64)), (1, 2, 64, 4.0)),
        "norm_gain": jnp.clip(1.0 + 0.18 * jax.random.normal(splits[1], (SECTIONS, D), jnp.float32), 0.1, 1.9),
        "weight_codes": touch_ends(jax.random.randint(splits[2], (SECTIONS, D, KV), -127, 128), jax.random.fold_in(splits[2], 1), -127, 127).astype(jnp.int32),
        "block_scales": jnp.clip(jnp.exp(math.log(0.0003) - 1.45528725 * jax.random.uniform(splits[3], (SECTIONS, D // BLOCK, KV), jnp.float32) ** shard_levels(splits[3], (SECTIONS, D // BLOCK, KV), ((0, 2), (1, 4)), -0.2, 0.2)), 7.000000186963007e-05, 0.0003),
        "value_grad": bell_draw(splits[4], (SECTIONS, TOKENS, KV), 3.0, 16.0, ((0, 2), (1, 64))),
    }


def dequantize(codes, scales):
    rows = codes.shape[0]
    cols = codes.shape[1]
    scaled = codes.astype(jnp.float32).reshape(rows // BLOCK, BLOCK, cols) * scales[:, None, :]
    return scaled.reshape(rows, cols).astype(jnp.bfloat16)

def reference(hidden_in, norm_gain, weight_codes, block_scales, value_grad):
    factor = float(TOKENS) ** (-0.5)
    value_list = []
    input_list = []
    grad_list = []
    for section_idx in range(SECTIONS):
        inputs = hidden_in[section_idx].astype(jnp.float32)
        gain_vec = norm_gain[section_idx]
        inv_rms = lax.rsqrt(lax.optimization_barrier(jnp.mean(inputs * inputs, axis=-1, keepdims=True)) + 1e-05)
        normed = (inputs * inv_rms * gain_vec).astype(jnp.bfloat16)
        weights = dequantize(weight_codes[section_idx], block_scales[section_idx])
        values = jnp.dot(normed, weights, preferred_element_type=jnp.float32).astype(jnp.bfloat16)
        cotan = value_grad[section_idx]
        normed_grad = lax.dot_general(cotan, weights, (((1,), (1,)), ((), ())), preferred_element_type=jnp.float32)
        scaled_grad = gain_vec * normed_grad
        inner = lax.optimization_barrier(jnp.mean(inputs * scaled_grad, axis=-1, keepdims=True))
        input_grad = (inv_rms * scaled_grad - inputs * inv_rms * inv_rms * inv_rms * inner).astype(jnp.bfloat16)
        normed_blocks = normed.reshape(N_DP, N_NODE, TOK_DEV, D)
        cotan_blocks = cotan.reshape(N_DP, N_NODE, TOK_DEV, KV)

        def over_nodes(total, node_idx):

            def over_dp(acc, dp_idx):
                term = lax.dot_general(normed_blocks[dp_idx, node_idx], cotan_blocks[dp_idx, node_idx], (((0,), (0,)), ((), ())), preferred_element_type=jnp.float32)
                term = (term * factor).astype(jnp.bfloat16).astype(jnp.float32)
                return (acc + term, None)
            group, unused = lax.scan(over_dp, jnp.zeros((D, KV), jnp.float32), jnp.arange(N_DP, dtype=jnp.int32))
            group = lax.optimization_barrier(group.astype(jnp.bfloat16))
            return (total + group.astype(jnp.float32), None)
        total, unused = lax.scan(over_nodes, jnp.zeros((D, KV), jnp.float32), jnp.arange(N_NODE, dtype=jnp.int32))
        value_list.append(values)
        input_list.append(input_grad)
        grad_list.append(total.astype(jnp.bfloat16))
    passed_values = jnp.roll(jnp.stack(value_list), 1, axis=0)
    return (passed_values, jnp.stack(input_list), jnp.stack(grad_list))
```

```python
import functools

import jax
import jax.numpy as jnp
from jax import lax
from jax.experimental import pallas as pl
from jax.experimental.pallas import tpu as pltpu
from jax.sharding import PartitionSpec as P

MESH = pl.DeviceIdType.MESH
BF16, F32 = jnp.bfloat16, jnp.float32
D, KV, TOK, NZ, NY = 8192, 1024, 256, 4, 4
SHARD = D // NZ
NB = 4
KB = KV // NB
BLK = 512
NBLK = D // BLK
FACTOR = 2.0 ** -7


def kernel(h_ref, gain_ref, codes_ref, scales_ref, cot_ref, pass_ref, ig_ref, wg_ref,
           hv, hs, cv, ct, nv, wall, cod, ng, part, y1, y2, xr, zr, vst, wgv, gv, sv, inv, cdv,
           l_sem, cod_sem, hs_s, hs_r, ct_s, ct_r, z_s, z_r, xw_s, xw_r, sw_s, sw_r,
           y1_s, y1_r, y2_s, y2_r, xr_s, xr_r, zr_s, zr_r, v_s, v_r, o_sem):
    sec, i, z = lax.axis_index("section"), lax.axis_index("dp"), lax.axis_index("node")
    x, y, c = i // 8, (i // 2) % 4, i % 2

    def dev(xx, yy, zz, cc, ss=None):
        return (sec if ss is None else ss, xx * 8 + yy * 2 + cc, zz)

    zp, zm, z2 = (z + 1) % 4, (z + 3) % 4, (z + 2) % 4
    yp, ym, yo = (y + 1) % 4, (y + 3) % 4, (y + 2) % 4
    d_sib, d_x = dev(x, y, z, 1 - c), dev(1 - x, y, z, c)
    d_yp, d_ym = dev(x, yp, z, c), dev(x, ym, z, c)
    d_z = [None, dev(x, y, zp, c), dev(x, y, z2, c), dev(x, y, zm, c)]
    d_sec = dev(x, y, z, c, 1 - sec)

    def remote(src, dst, s, r, device):
        return pltpu.make_async_remote_copy(src_ref=src, dst_ref=dst, send_sem=s, recv_sem=r,
                                            device_id=device, device_id_type=MESH)

    def load_h(b):
        return pltpu.make_async_copy(h_ref.at[0, :, pl.ds(pl.multiple_of(b * BLK, BLK), BLK)], hv.at[b], l_sem.at[b])

    def load_codes(kb):
        return pltpu.make_async_copy(codes_ref.at[0, :, pl.ds(kb * KB, KB)], cod.at[kb % 2], cod_sem.at[kb])

    cp_g = pltpu.make_async_copy(gain_ref, gv, l_sem.at[NBLK])
    cp_s = pltpu.make_async_copy(scales_ref.at[0], sv, l_sem.at[NBLK + 1])
    cp_c = pltpu.make_async_copy(cot_ref.at[0], cv, l_sem.at[NBLK + 2])
    cp_s.start()
    load_codes(0).start()
    load_codes(1).start()
    cp_c.start()
    cp_g.start()

    @pl.loop(0, NBLK)
    def _(b):
        load_h(b).start()

    barrier = pltpu.get_barrier_semaphore()
    for target in (d_sib, d_x, d_yp, d_ym, d_z[1], d_z[2], d_z[3], d_sec):
        pl.semaphore_signal(barrier, inc=1, device_id=target, device_id_type=MESH)
    pl.semaphore_wait(barrier, 8)

    def send_h(e):
        col = pl.multiple_of(e * (2 * BLK) + (1 - c) * BLK, BLK)
        return remote(h_ref.at[0, :, pl.ds(col, BLK)], hs.at[e], hs_s.at[e], hs_r.at[e], d_sib)

    @pl.loop(0, 8)
    def _(e):
        send_h(e).start()

    r0 = pl.multiple_of(c * 1024 + x * 256, 256)
    q0 = pl.multiple_of(c * 1024 + x * 768, 256)

    def z_copy(kb, k):
        if k == 0:
            ref = wall.at[kb, z, pl.ds(r0, 768)]
            return remote(ref, ref, z_s.at[kb, 0], z_r.at[kb, 0], d_z[1])
        if k == 1:
            ref = wall.at[kb, z, pl.ds(r0, 768)]
            return remote(ref, ref, z_s.at[kb, 1], z_r.at[kb, 1], d_z[3])
        if k == 2:
            ref = wall.at[kb, zm, pl.ds(r0, 384)]
            return remote(ref, ref, z_s.at[kb, 2], z_r.at[kb, 2], d_z[1])
        ref = wall.at[kb, zp, pl.ds(r0 + 384, 384)]
        return remote(ref, ref, z_s.at[kb, 3], z_r.at[kb, 3], d_z[3])

    shards = (zm, zp, z2)

    def x_copy(kb, k):
        ref = wall.at[kb, shards[k], pl.ds(q0, 256)]
        return remote(ref, ref, xw_s.at[kb, k], xw_r.at[kb, k], d_x)

    def sib_copy(kb, k):
        if k < 3:
            ref = wall.at[kb, shards[k], pl.ds(r0, 768)]
        else:
            ref = wall.at[kb, shards[k - 3], pl.ds(pl.multiple_of(c * 1024 + (1 - x) * 768, 256), 256)]
        return remote(ref, ref, sw_s.at[kb, k], sw_r.at[kb, k], d_sib)

    def dequant(kb):
        load_codes(kb).wait()

        @pl.loop(0, SHARD // 256)
        def _(g):
            rows = pl.ds(pl.multiple_of(g * 256, 256), 256)
            scale = sv[pl.ds(g, 1), kb * KB:(kb + 1) * KB]
            wall[kb, z, rows, :] = (cod[kb % 2, rows, :].astype(F32) * scale).astype(BF16)

        if kb + 2 < NB:
            load_codes(kb + 2).start()
        z_copy(kb, 0).start()
        z_copy(kb, 1).start()

    cp_s.wait()
    dequant(0)
    dequant(1)

    @pl.loop(0, NBLK)
    def _(b):
        load_h(b).wait()

    def squares(b, acc):
        v = hv[b].astype(F32)
        v = v * v
        return acc + v[:, 0:128] + v[:, 128:256] + v[:, 256:384] + v[:, 384:512]

    acc = lax.fori_loop(0, NBLK, squares, jnp.zeros((TOK, 128), F32))
    inv[...] = jnp.broadcast_to(lax.rsqrt(jnp.sum(acc, axis=1, keepdims=True) * (1.0 / D) + 1e-05), (TOK, 128))

    cp_c.wait()
    for q in range(4):
        scaled = cv[:, q * 256:(q + 1) * 256].astype(F32) * inv[:, 0:1]
        ct[0, q * 256:(q + 1) * 256, :] = jnp.transpose(scaled).astype(BF16)
    send_ct = remote(ct.at[0], ct.at[1], ct_s.at[0], ct_r.at[0], d_sib)
    send_ct.start()

    cp_g.wait()

    @pl.loop(0, NBLK)
    def _(b):
        g = gv[0:1, pl.ds(pl.multiple_of(b * BLK, BLK), BLK)]
        nv[b] = (hv[b].astype(F32) * inv[:, 0:1] * g).astype(BF16)

    @pl.loop(0, 8)
    def _(e):
        send_h(e).wait_recv()

    send_ct.wait_recv()

    def term(xx, yy):
        own = hv.at[xx * 8 + yy * 2 + c]
        other = hs.at[xx * 4 + yy]

        @pl.loop(0, 4)
        def _(q):
            rows = pl.ds(pl.multiple_of(q * 256, 256), 256)
            t = jnp.dot(ct[0, rows, :], own[...], preferred_element_type=F32)
            t = t + jnp.dot(ct[1, rows, :], other[...], preferred_element_type=F32)
            part[xx, yy, q] = (t * FACTOR).astype(BF16)

    def unit(u):
        n, q = u // 4, u % 4
        return (x + 1 + n) % 2, q

    def y1_copy(u, k):
        xx, q = unit(u)
        return remote(part.at[xx, yo, q, pl.ds(k * 128, 128)], y1.at[u, k], y1_s.at[u, k], y1_r.at[u, k],
                      (d_yp, d_ym)[k])

    def y2_copy(u, k):
        xx, q = unit(u)
        return remote(part.at[xx, (yp, ym)[k], q], y2.at[u, k], y2_s.at[u, k], y2_r.at[u, k], (d_yp, d_ym)[k])

    def xr_copy(q):
        return remote(part.at[1 - x, y, q], xr.at[q], xr_s.at[q], xr_r.at[q], d_x)

    def zr_copy(q, m):
        cols = pl.ds(pl.multiple_of(((z + m) % 4) * 128, 128), 128)
        return remote(part.at[x, y, q, :, cols], zr.at[q, m - 1], zr_s.at[q, m - 1], zr_r.at[q, m - 1], d_z[m])

    @pl.loop(0, 2)
    def _(n):
        term((x + 1 + n) % 2, yo)

        @pl.loop(0, 4)
        def _(q):
            y1_copy(n * 4 + q, 0).start()
            y1_copy(n * 4 + q, 1).start()

    @pl.loop(0, 2)
    def _(n):
        term((x + 1 + n) % 2, yp)
        term((x + 1 + n) % 2, ym)

    @pl.loop(0, 2)
    def _(n):
        term((x + 1 + n) % 2, y)

    def grad_a(lo, hi):
        @pl.loop(lo, hi)
        def _(u):
            xx, q = unit(u)
            y1_copy(u, 0).wait_recv()
            part[xx, yp, q, 0:128, :] = (part[xx, yp, q, 0:128, :].astype(F32) + y1[u, 0].astype(F32)).astype(BF16)
            y2_copy(u, 0).start()
            y1_copy(u, 1).wait_recv()
            part[xx, ym, q, 128:256, :] = (part[xx, ym, q, 128:256, :].astype(F32) + y1[u, 1].astype(F32)).astype(BF16)
            y2_copy(u, 1).start()

    def grad_b0(lo, hi):
        @pl.loop(lo, hi)
        def _(q):
            y2_copy(q, 0).wait_recv()
            y2_copy(q, 1).wait_recv()
            part[1 - x, y, q] = (part[1 - x, y, q].astype(F32) + y2[q, 0].astype(F32)
                                 + y2[q, 1].astype(F32)).astype(BF16)
            xr_copy(q).start()

    def grad_b1(lo, hi):
        @pl.loop(lo, hi)
        def _(q):
            xr_copy(q).wait_recv()
            y2_copy(4 + q, 0).wait_recv()
            y2_copy(4 + q, 1).wait_recv()
            part[x, y, q] = (part[x, y, q].astype(F32) + y2[4 + q, 0].astype(F32) + y2[4 + q, 1].astype(F32)
                             + xr[q].astype(F32)).astype(BF16)
            for m in (1, 2, 3):
                zr_copy(q, m).start()

    d0 = pl.multiple_of(i * 512 + z * 128, 128)

    def grad_c(q):
        for m in (1, 2, 3):
            zr_copy(q, m).wait_recv()
        own = part[x, y, q, :, pl.ds(pl.multiple_of(z * 128, 128), 128)].astype(F32)
        total = own + zr[q, 0].astype(F32) + zr[q, 1].astype(F32) + zr[q, 2].astype(F32)
        total = total * gv[0:1, pl.ds(d0, 128)]
        wgv[:, q * 256:(q + 1) * 256] = jnp.transpose(total).astype(BF16)

    def w_a(kb):
        z_copy(kb, 0).wait_recv()
        z_copy(kb, 2).start()
        x_copy(kb, 0).start()
        sib_copy(kb, 0).start()
        z_copy(kb, 1).wait_recv()
        z_copy(kb, 3).start()
        x_copy(kb, 1).start()
        sib_copy(kb, 1).start()

    def w_b(kb):
        z_copy(kb, 2).wait_recv()
        z_copy(kb, 3).wait_recv()
        x_copy(kb, 2).start()
        sib_copy(kb, 2).start()

    def w_c(kb):
        for k in range(3):
            x_copy(kb, k).wait_recv()
            sib_copy(kb, 3 + k).start()

    def pass_copy(kb):
        return remote(vst.at[kb], pass_ref.at[0, :, pl.ds(kb * KB, KB)], v_s.at[kb], v_r.at[kb], d_sec)

    def out_copy(b):
        return pltpu.make_async_copy(nv.at[b], ig_ref.at[0, :, pl.ds(pl.multiple_of(b * BLK, BLK), BLK)], o_sem.at[b])

    def w_d(kb):
        for k in range(6):
            sib_copy(kb, k).wait_recv()
        cols = slice(kb * KB, (kb + 1) * KB)
        last = kb == NB - 1

        def weight(b):
            return wall[kb, b // 4, pl.ds(pl.multiple_of((b % 4) * BLK, BLK), BLK), :]

        def grad_of(b):
            return lax.dot_general(cv[:, cols], weight(b), (((1,), (1,)), ((), ())), preferred_element_type=F32)

        def step(b, acc):
            w = weight(b)
            if not last:
                t = grad_of(b)
                if kb == 0:
                    ng[b] = t
                else:
                    ng[b] = ng[b] + t
            return acc + jnp.dot(nv[b], w, preferred_element_type=F32)

        vals = lax.fori_loop(0, NBLK, step, jnp.zeros((TOK, KB), F32))
        vst[kb] = vals.astype(BF16)
        pass_copy(kb).start()
        prod = vals * cv[:, cols].astype(F32)
        prod = prod[:, 0:128] + prod[:, 128:256]
        if kb == 0:
            cdv[...] = prod
        else:
            cdv[...] = cdv[...] + prod
        if last:
            iv = inv[:, 0:1]
            coef = iv * iv * (jnp.sum(cdv[...], axis=1, keepdims=True) * (1.0 / D))

            @pl.loop(0, NBLK)
            def _(b):
                g = gv[0:1, pl.ds(pl.multiple_of(b * BLK, BLK), BLK)]
                t = ng[b] + grad_of(b)
                nv[b] = (iv * g * t - hv[b].astype(F32) * coef).astype(BF16)
                out_copy(b).start()

    w_a(0)
    grad_a(0, 4)
    w_a(1)
    dequant(2)
    w_b(0)
    w_c(0)
    grad_a(4, 8)
    w_d(0)
    w_a(2)
    dequant(3)
    w_b(1)
    w_c(1)
    grad_b0(0, 1)
    w_d(1)
    w_a(3)
    grad_b0(1, 3)
    w_b(2)
    w_c(2)
    w_d(2)
    w_b(3)
    w_c(3)
    w_d(3)
    grad_b0(3, 4)
    grad_b1(0, 2)
    grad_c(0)
    grad_b1(2, 3)
    grad_c(1)
    grad_b1(3, 4)
    grad_c(2)
    grad_c(3)
    cp_w = pltpu.make_async_copy(wgv, wg_ref.at[0], l_sem.at[NBLK + 3])
    cp_w.start()

    @pl.loop(0, 8)
    def _(e):
        send_h(e).wait_send()
        for k in range(2):
            y1_copy(e, k).wait_send()
            y2_copy(e, k).wait_send()

    send_ct.wait_send()

    @pl.loop(0, 4)
    def _(q):
        xr_copy(q).wait_send()
        for m in (1, 2, 3):
            zr_copy(q, m).wait_send()

    for kb in range(NB):
        for k in range(4):
            z_copy(kb, k).wait_send()
        for k in range(3):
            x_copy(kb, k).wait_send()
        for k in range(6):
            sib_copy(kb, k).wait_send()
        pass_copy(kb).wait()

    @pl.loop(0, NBLK)
    def _(b):
        out_copy(b).wait()

    cp_w.wait()


def on_device(hidden_in, norm_gain, weight_codes, block_scales, value_grad):
    dma, any_ = pltpu.SemaphoreType.DMA, pl.BlockSpec(memory_space=pl.ANY)
    v = pltpu.VMEM
    return pl.pallas_call(
        kernel,
        out_shape=(
            jax.ShapeDtypeStruct((1, TOK, KV), BF16),
            jax.ShapeDtypeStruct((1, TOK, D), BF16),
            jax.ShapeDtypeStruct((1, 128, KV), BF16),
        ),
        in_specs=[any_] * 5,
        out_specs=[any_] * 3,
        scratch_shapes=[
            v((NBLK, TOK, BLK), BF16),
            v((8, TOK, BLK), BF16),
            v((TOK, KV), BF16),
            v((2, KV, TOK), BF16),
            v((NBLK, TOK, BLK), BF16),
            v((NB, NZ, SHARD, KB), BF16),
            v((2, SHARD, KB), jnp.int32),
            v((NBLK, TOK, BLK), F32),
            v((2, NY, 4, 256, BLK), BF16),
            v((8, 2, 128, BLK), BF16),
            v((8, 2, 256, BLK), BF16),
            v((4, 256, BLK), BF16),
            v((4, 3, 256, 128), BF16),
            v((NB, TOK, KB), BF16),
            v((128, KV), BF16),
            v((1, D), F32),
            v((8, KV), F32),
            v((TOK, 128), F32),
            v((TOK, 128), F32),
            dma((NBLK + 4,)), dma((NB,)),
            dma((8,)), dma((8,)), dma((1,)), dma((1,)),
            dma((NB, 4)), dma((NB, 4)), dma((NB, 3)), dma((NB, 3)), dma((NB, 6)), dma((NB, 6)),
            dma((8, 2)), dma((8, 2)), dma((8, 2)), dma((8, 2)),
            dma((4,)), dma((4,)), dma((4, 3)), dma((4, 3)), dma((NB,)), dma((NB,)), dma((NBLK,)),
        ],
        compiler_params=pltpu.CompilerParams(
            collective_id=0, has_side_effects=True, vmem_limit_bytes=63 * 2 ** 20),
        cost_estimate=pl.CostEstimate(flops=3 * 2 * TOK * D * KV, bytes_accessed=24 * 2 ** 20, transcendentals=TOK),
    )(hidden_in, norm_gain, weight_codes, block_scales, value_grad)


def solution(mesh):
    return jax.shard_map(
        on_device,
        mesh=mesh,
        in_specs=(
            P("section", ("dp", "node"), None),
            P("section", None),
            P("section", "node", None),
            P("section", "node", None),
            P("section", ("dp", "node"), None),
        ),
        out_specs=(
            P("section", ("dp", "node"), None),
            P("section", ("dp", "node"), None),
            P("section", ("dp", "node"), None),
        ),
        check_vma=False,
    )
```

```python
import functools

import jax
import jax.numpy as jnp
from jax import lax
from jax.experimental import pallas as pl
from jax.experimental.pallas import tpu as pltpu
from jax.sharding import PartitionSpec as P

MESH = pl.DeviceIdType.MESH
BF16, F32 = jnp.bfloat16, jnp.float32
D, KV, TOK, NZ, NY = 8192, 1024, 256, 4, 4
SHARD = D // NZ
NB = 4
KB = KV // NB
BLK = 512
NBLK = D // BLK
FACTOR = 2.0 ** -7
QR = 192
UN = 8
UR = KV // UN
PR = 1024 - 2 * QR


def kernel(h_ref, gain_ref, codes_ref, scales_ref, cot_ref, pass_ref, ig_ref, wg_ref,
           hv, cv, ct, nv, wall, cod, ng, part, y1, y2, xr, zr, vst, wgv, gv, sv, inv, cdv,
           l_sem, cod_sem, hs_s, hs_r, ct_s, ct_r, z_s, z_r, xw_s, xw_r, sw_s, sw_r,
           y1_s, y1_r, y2_s, y2_r, xr_s, xr_r, zr_s, zr_r, v_s, v_r, o_sem):
    sec, i, z = lax.axis_index("section"), lax.axis_index("dp"), lax.axis_index("node")
    x, y, c = i // 8, (i // 2) % 4, i % 2

    def dev(xx, yy, zz, cc, ss=None):
        return (sec if ss is None else ss, xx * 8 + yy * 2 + cc, zz)

    zp, zm, z2 = (z + 1) % 4, (z + 3) % 4, (z + 2) % 4
    yp, ym, yo = (y + 1) % 4, (y + 3) % 4, (y + 2) % 4
    d_sib, d_x = dev(x, y, z, 1 - c), dev(1 - x, y, z, c)
    d_yp, d_ym = dev(x, yp, z, c), dev(x, ym, z, c)
    d_z = [None, dev(x, y, zp, c), dev(x, y, z2, c), dev(x, y, zm, c)]
    d_sec = dev(x, y, z, c, 1 - sec)

    def remote(src, dst, s, r, device):
        return pltpu.make_async_remote_copy(src_ref=src, dst_ref=dst, send_sem=s, recv_sem=r,
                                            device_id=device, device_id_type=MESH)

    def load_h(e, k):
        bit = c if k == 0 else 1 - c
        col = pl.multiple_of(e * (2 * BLK) + bit * BLK, BLK)
        return pltpu.make_async_copy(h_ref.at[0, :, pl.ds(col, BLK)], hv.at[e, k], l_sem.at[e * 2 + k // 2])

    def load_codes(kb):
        return pltpu.make_async_copy(codes_ref.at[0, :, pl.ds(kb * KB, KB)], cod.at[kb % 2], cod_sem.at[kb])

    barrier = pltpu.get_barrier_semaphore()
    for target in (d_sib, d_x, d_yp, d_ym, d_z[1], d_z[2], d_z[3], d_sec):
        pl.semaphore_signal(barrier, inc=1, device_id=target, device_id_type=MESH)

    cp_g = pltpu.make_async_copy(gain_ref, gv, l_sem.at[NBLK])
    cp_s = pltpu.make_async_copy(scales_ref.at[0], sv, l_sem.at[NBLK + 1])
    cp_c = pltpu.make_async_copy(cot_ref.at[0], cv, l_sem.at[NBLK + 2])
    cp_s.start()
    load_codes(0).start()

    @pl.loop(0, 8)
    def _(e):
        load_h(e, 0).start()
        load_h(e, 2).start()

    cp_c.start()
    load_codes(1).start()
    cp_g.start()

    def send_h(e):
        col = pl.multiple_of(e * (2 * BLK) + (1 - c) * BLK, BLK)
        return remote(h_ref.at[0, :, pl.ds(col, BLK)], hv.at[e, 1], hs_s.at[e], hs_r.at[e], d_sib)

    base = c * 1024
    p0 = pl.multiple_of(base + QR, 32)
    q0 = pl.multiple_of(base + x * (QR + PR), 32)
    q1 = pl.multiple_of(base + (1 - x) * (QR + PR), 32)
    r0 = pl.multiple_of(base + x * QR, 32)

    def z_copy(kb, k):
        start, size = (q0, QR) if k < 4 else (p0, PR)
        if k % 4 < 2:
            ref = wall.at[kb, z, pl.ds(start, size)]
        elif k % 4 == 2:
            ref = wall.at[kb, zm, pl.ds(start, size // 2)]
        else:
            ref = wall.at[kb, zp, pl.ds(pl.multiple_of(start + size // 2, 16), size // 2)]
        return remote(ref, ref, z_s.at[kb, k], z_r.at[kb, k], d_z[1 if k % 2 == 0 else 3])

    shards = (zm, zp, z2)

    def x_copy(kb, k):
        ref = wall.at[kb, shards[k], pl.ds(q0, QR)]
        return remote(ref, ref, xw_s.at[kb, k], xw_r.at[kb, k], d_x)

    def sib_copy(kb, k):
        if k < 3:
            ref = wall.at[kb, shards[k], pl.ds(r0, PR + QR)]
        else:
            ref = wall.at[kb, shards[k - 3], pl.ds(q1, QR)]
        return remote(ref, ref, sw_s.at[kb, k], sw_r.at[kb, k], d_sib)

    def dequant(kb):
        load_codes(kb).wait()

        @pl.loop(0, SHARD // 256)
        def _(g):
            rows = pl.ds(pl.multiple_of(g * 256, 256), 256)
            scale = sv[pl.ds(g, 1), kb * KB:(kb + 1) * KB]
            wall[kb, z, rows, :] = (cod[kb % 2, rows, :].astype(F32) * scale).astype(BF16)

        if kb + 2 < NB:
            load_codes(kb + 2).start()

    def w_send(kb):
        for k in (0, 1, 4, 5):
            z_copy(kb, k).start()

    cp_s.wait()
    dequant(0)
    pl.semaphore_wait(barrier, 8)

    @pl.loop(0, 8)
    def _(e):
        send_h(e).start()

    w_send(0)

    @pl.loop(0, 8)
    def _(e):
        load_h(e, 0).wait()
        load_h(e, 2).wait()

    def squares(e, acc):
        for k in (0, 2):
            v = hv[e, k].astype(F32)
            v = v * v
            acc = acc + (v[:, 0:128] + v[:, 128:256]) + (v[:, 256:384] + v[:, 384:512])
        return acc

    acc = lax.fori_loop(0, 8, squares, jnp.zeros((TOK, 128), F32))
    inv[...] = jnp.broadcast_to(lax.rsqrt(jnp.sum(acc, axis=1, keepdims=True) * (1.0 / D) + 1e-05), (TOK, 128))

    cp_c.wait()
    for q in range(4):
        scaled = cv[:, q * 256:(q + 1) * 256].astype(F32) * inv[:, 0:1]
        ct[q * 256:(q + 1) * 256, 0:256] = jnp.transpose(scaled).astype(BF16)
    send_ct = remote(ct.at[:, pl.ds(0, 256)], ct.at[:, pl.ds(256, 256)], ct_s.at[0], ct_r.at[0], d_sib)
    send_ct.start()
    cp_g.wait()
    dequant(1)
    w_send(1)

    @pl.loop(0, 8)
    def _(e):
        send_h(e).wait_recv()

    send_ct.wait_recv()

    def term(xx, yy):
        both = hv[xx * 4 + yy, 0:2].reshape(2 * TOK, BLK)

        for lo in (0, 256):
            t = jnp.dot(ct[...], both[:, lo:lo + 256], preferred_element_type=F32)
            part[xx, yy, :, :, lo:lo + 256] = (t * FACTOR).astype(BF16).reshape(UN, UR, 256)

    def row(n):
        return (x + 1 + n) % 2

    def y1_copy(n, q, k):
        return remote(part.at[row(n), yo, q, pl.ds(k * (UR // 2), UR // 2)], y1.at[n, q, k],
                      y1_s.at[n, q, k], y1_r.at[n, q, k], (d_yp, d_ym)[k])

    def y2_copy(n, q, k):
        return remote(part.at[row(n), (yp, ym)[k], q], y2.at[n, q, k], y2_s.at[n, q, k], y2_r.at[n, q, k],
                      (d_yp, d_ym)[k])

    def xr_copy(q):
        return remote(part.at[1 - x, y, q], xr.at[q], xr_s.at[q], xr_r.at[q], d_x)

    def zr_copy(q, m):
        cols = pl.ds(pl.multiple_of(((z + m) % 4) * 128, 128), 128)
        return remote(part.at[x, y, q, :, cols], zr.at[q, m - 1], zr_s.at[q, m - 1], zr_r.at[q, m - 1], d_z[m])

    def y1_send(n):
        term(row(n), yo)

        @pl.loop(0, UN)
        def _(q):
            y1_copy(n, q, 0).start()
            y1_copy(n, q, 1).start()

    def terms(n):
        for yy in (yp, ym):
            term(row(n), yy)

    def grad_a(n, q, k):
        xx, yy = row(n), (yp, ym)[k]
        rows = slice(k * (UR // 2), (k + 1) * (UR // 2))
        y1_copy(n, q, k).wait_recv()
        part[xx, yy, q, rows, :] = (part[xx, yy, q, rows, :].astype(F32) + y1[n, q, k].astype(F32)).astype(BF16)
        y2_copy(n, q, k).start()

    def y_sum(n, q):
        y2_copy(n, q, 0).wait_recv()
        y2_copy(n, q, 1).wait_recv()
        return part[row(n), y, q].astype(F32) + y2[n, q, 0].astype(F32) + y2[n, q, 1].astype(F32)

    def grad_b0(q):
        part[1 - x, y, q] = y_sum(0, q).astype(BF16)
        xr_copy(q).start()

    def grad_b1(q):
        xr_copy(q).wait_recv()
        part[x, y, q] = (y_sum(1, q) + xr[q].astype(F32)).astype(BF16)
        for m in (1, 3, 2):
            zr_copy(q, m).start()

    d0 = pl.multiple_of(i * 512 + z * 128, 128)

    def grad_c(q):
        for m in (1, 2, 3):
            zr_copy(q, m).wait_recv()
        own = part[x, y, q, :, pl.ds(pl.multiple_of(z * 128, 128), 128)].astype(F32)
        total = own + zr[q, 0].astype(F32) + zr[q, 1].astype(F32) + zr[q, 2].astype(F32)
        total = total * gv[0:1, pl.ds(d0, 128)]
        wgv[:, q * UR:(q + 1) * UR] = jnp.transpose(total).astype(BF16)

    def w_q(kb, k):
        z_copy(kb, k).wait_recv()
        z_copy(kb, 2 + k).start()
        x_copy(kb, k).start()

    def w_p(kb, k):
        z_copy(kb, 4 + k).wait_recv()
        z_copy(kb, 6 + k).start()
        sib_copy(kb, k).start()

    def w_bq(kb):
        z_copy(kb, 2).wait_recv()
        z_copy(kb, 3).wait_recv()
        x_copy(kb, 2).start()

    def w_bp(kb):
        z_copy(kb, 6).wait_recv()
        z_copy(kb, 7).wait_recv()
        sib_copy(kb, 2).start()

    def w_c(kb, k):
        x_copy(kb, k).wait_recv()
        sib_copy(kb, 3 + k).start()

    def pass_copy(kb):
        return remote(vst.at[kb], pass_ref.at[0, :, pl.ds(kb * KB, KB)], v_s.at[kb], v_r.at[kb], d_sec)

    def out_copy(zz):
        return pltpu.make_async_copy(nv.at[zz], ig_ref.at[0, :, pl.ds(pl.multiple_of(zz * SHARD, SHARD), SHARD)],
                                     o_sem.at[zz])

    def h_block(zz, r):
        return hv[zz * 2 + r // 2, jnp.where(c == r % 2, 0, 2)].astype(F32)

    def gain_block(zz, r):
        return gv[0:1, pl.ds(pl.multiple_of(zz * SHARD + r * BLK, BLK), BLK)]

    def normalize():
        @pl.loop(0, NZ)
        def _(zz):
            for r in range(4):
                nv[zz, :, r * BLK:(r + 1) * BLK] = (h_block(zz, r) * inv[:, 0:1] * gain_block(zz, r)).astype(BF16)

    def grad_of(kb, zz, lo, size):
        return lax.dot_general(cv[:, kb * KB:(kb + 1) * KB], wall[kb, zz, lo:lo + size, :], (((1,), (1,)), ((), ())),
                               preferred_element_type=F32)

    def w_d(kb):
        for k in range(6):
            sib_copy(kb, k).wait_recv()
        cols = slice(kb * KB, (kb + 1) * KB)
        last = kb == NB - 1

        def step(zz, acc):
            if not last:
                for lo in (0, 1024):
                    t = grad_of(kb, zz, lo, 1024)
                    if kb == 0:
                        ng[zz, :, lo:lo + 1024] = t
                    else:
                        ng[zz, :, lo:lo + 1024] = ng[zz, :, lo:lo + 1024] + t
            return acc + jnp.dot(nv[zz], wall[kb, zz], preferred_element_type=F32)

        vals = lax.fori_loop(0, NZ, step, jnp.zeros((TOK, KB), F32))
        vst[kb] = vals.astype(BF16)
        pass_copy(kb).start()
        prod = vals * cv[:, cols].astype(F32)
        prod = prod[:, 0:128] + prod[:, 128:256]
        if kb == 0:
            cdv[...] = prod
        else:
            cdv[...] = cdv[...] + prod

    def w_e():
        kb = NB - 1
        iv = inv[:, 0:1]
        coef = iv * iv * (jnp.sum(cdv[...], axis=1, keepdims=True) * (1.0 / D))

        @pl.loop(0, NZ)
        def _(zz):
            for r in range(4):
                lanes = slice(r * BLK, (r + 1) * BLK)
                t = ng[zz, :, lanes] + grad_of(kb, zz, r * BLK, BLK)
                nv[zz, :, lanes] = (iv * gain_block(zz, r) * t - h_block(zz, r) * coef).astype(BF16)
            out_copy(zz).start()

    y1_send(0)
    y1_send(1)
    w_q(0, 0)
    w_q(0, 1)
    dequant(2)
    w_send(2)
    dequant(3)
    w_send(3)
    terms(0)
    w_q(1, 0)
    w_q(1, 1)
    w_p(0, 0)
    w_p(0, 1)
    w_c(0, 0)
    grad_a(0, 0, 0)
    grad_a(0, 0, 1)
    grad_a(0, 1, 0)
    grad_a(0, 1, 1)
    grad_a(0, 2, 0)
    grad_a(0, 2, 1)
    grad_a(0, 3, 0)
    grad_a(0, 3, 1)
    w_c(0, 1)
    grad_a(0, 4, 0)
    grad_a(0, 4, 1)
    terms(1)
    w_c(1, 0)
    grad_a(0, 5, 0)
    grad_a(0, 5, 1)
    grad_a(0, 6, 0)
    grad_a(0, 6, 1)
    term(row(0), y)
    grad_a(0, 7, 0)
    w_c(1, 1)
    grad_a(0, 7, 1)
    term(row(1), y)
    w_p(1, 0)
    w_p(1, 1)
    grad_a(1, 0, 0)
    grad_a(1, 0, 1)
    w_bq(0)
    normalize()
    grad_a(1, 1, 0)
    grad_a(1, 1, 1)
    grad_a(1, 2, 0)
    w_q(2, 0)
    w_q(2, 1)
    grad_a(1, 2, 1)
    grad_a(1, 3, 0)
    grad_a(1, 3, 1)
    w_c(0, 2)
    grad_a(1, 4, 0)
    grad_a(1, 4, 1)
    w_c(2, 0)
    grad_a(1, 5, 0)
    grad_a(1, 5, 1)
    grad_a(1, 6, 0)
    grad_a(1, 6, 1)
    w_c(2, 1)
    grad_a(1, 7, 0)
    w_p(2, 0)
    w_p(2, 1)
    grad_a(1, 7, 1)
    w_q(3, 0)
    w_q(3, 1)
    grad_b0(0)
    grad_b0(1)
    w_c(3, 0)
    w_c(3, 1)
    grad_b0(2)
    w_p(3, 0)
    w_p(3, 1)
    w_bq(1)
    grad_b0(3)
    w_bp(0)
    grad_b0(4)
    w_d(0)
    w_bq(2)
    w_bp(1)
    w_c(1, 2)
    grad_b0(5)
    grad_b0(6)
    w_d(1)
    w_bq(3)
    w_bp(2)
    grad_b0(7)
    grad_b1(0)
    w_bp(3)
    grad_b1(1)
    w_c(2, 2)
    grad_c(0)
    w_d(2)
    grad_b1(2)
    grad_b1(3)
    grad_c(1)
    grad_b1(4)
    grad_c(2)
    grad_c(3)
    grad_b1(5)
    w_c(3, 2)
    w_d(3)
    grad_b1(6)
    grad_c(4)
    w_e()
    grad_b1(7)
    grad_c(5)
    grad_c(6)
    grad_c(7)
    cp_w = pltpu.make_async_copy(wgv, wg_ref.at[0], l_sem.at[NBLK + 3])
    cp_w.start()

    @pl.loop(0, 8)
    def _(e):
        send_h(e).wait_send()

    send_ct.wait_send()

    @pl.loop(0, UN)
    def _(q):
        for n in range(2):
            for k in range(2):
                y1_copy(n, q, k).wait_send()
                y2_copy(n, q, k).wait_send()
        xr_copy(q).wait_send()
        for m in (1, 2, 3):
            zr_copy(q, m).wait_send()

    for kb in range(NB):
        for k in range(8):
            z_copy(kb, k).wait_send()
        for k in range(3):
            x_copy(kb, k).wait_send()
        for k in range(6):
            sib_copy(kb, k).wait_send()
        pass_copy(kb).wait()

    for zz in range(NZ):
        out_copy(zz).wait()

    cp_w.wait()


def hand_over(a_in, b_in, c_in, a_out, b_out, c_out, a_v, b_v, c_v, sem_in, sem_out):
    refs = [(a_in.at[0], a_v, a_out.at[0]), (c_in.at[0], c_v, c_out.at[0])]
    for k in range(8):
        rows = pl.ds(k * 32, 32)
        refs.append((b_in.at[0, rows], b_v.at[rows], b_out.at[0, rows]))
    first = [pltpu.make_async_copy(a, b, sem_in.at[k]) for k, (a, b, _) in enumerate(refs)]
    second = [pltpu.make_async_copy(b, d, sem_out.at[k]) for k, (_, b, d) in enumerate(refs)]
    for copy in first:
        copy.start()
    for one, two in zip(first, second):
        one.wait()
        two.start()
    for copy in second:
        copy.wait()


def on_device(hidden_in, norm_gain, weight_codes, block_scales, value_grad):
    dma, any_ = pltpu.SemaphoreType.DMA, pl.BlockSpec(memory_space=pl.ANY)
    v = pltpu.VMEM
    out = pl.pallas_call(
        kernel,
        out_shape=(
            jax.ShapeDtypeStruct((1, TOK, KV), BF16),
            jax.ShapeDtypeStruct((1, TOK, D), BF16),
            jax.ShapeDtypeStruct((1, 128, KV), BF16),
        ),
        in_specs=[any_] * 5,
        out_specs=[any_] * 3,
        scratch_shapes=[
            v((8, 3, TOK, BLK), BF16),
            v((TOK, KV), BF16),
            v((KV, 2 * TOK), BF16),
            v((NZ, TOK, SHARD), BF16),
            v((NB, NZ, SHARD, KB), BF16),
            v((2, SHARD, KB), jnp.int32),
            v((NZ, TOK, SHARD), F32),
            v((2, NY, UN, UR, BLK), BF16),
            v((2, UN, 2, UR // 2, BLK), BF16),
            v((2, UN, 2, UR, BLK), BF16),
            v((UN, UR, BLK), BF16),
            v((UN, 3, UR, 128), BF16),
            v((NB, TOK, KB), BF16),
            v((128, KV), BF16),
            v((1, D), F32),
            v((8, KV), F32),
            v((TOK, 128), F32),
            v((TOK, 128), F32),
            dma((NBLK + 4,)), dma((NB,)),
            dma((8,)), dma((8,)), dma((1,)), dma((1,)),
            dma((NB, 8)), dma((NB, 8)), dma((NB, 3)), dma((NB, 3)), dma((NB, 6)), dma((NB, 6)),
            dma((2, UN, 2)), dma((2, UN, 2)), dma((2, UN, 2)), dma((2, UN, 2)),
            dma((UN,)), dma((UN,)), dma((UN, 3)), dma((UN, 3)), dma((NB,)), dma((NB,)), dma((NZ,)),
        ],
        compiler_params=pltpu.CompilerParams(
            collective_id=0, has_side_effects=True, vmem_limit_bytes=63 * 2 ** 20),
        cost_estimate=pl.CostEstimate(flops=3 * 2 * TOK * D * KV, bytes_accessed=24 * 2 ** 20, transcendentals=TOK),
    )(hidden_in, norm_gain, weight_codes, block_scales, value_grad)
    return pl.pallas_call(
        hand_over,
        out_shape=tuple(jax.ShapeDtypeStruct(o.shape, o.dtype) for o in out),
        in_specs=[any_] * 3,
        out_specs=[any_] * 3,
        scratch_shapes=[v((TOK, KV), BF16), v((TOK, D), BF16), v((128, KV), BF16), dma((10,)), dma((10,))],
    )(*out)


def solution(mesh):
    return jax.shard_map(
        on_device,
        mesh=mesh,
        in_specs=(
            P("section", ("dp", "node"), None),
            P("section", None),
            P("section", "node", None),
            P("section", "node", None),
            P("section", ("dp", "node"), None),
        ),
        out_specs=(
            P("section", ("dp", "node"), None),
            P("section", ("dp", "node"), None),
            P("section", ("dp", "node"), None),
        ),
        check_vma=False,
    )
```

```python
import functools

import jax
import jax.numpy as jnp
from jax import lax
from jax.experimental import pallas as pl
from jax.experimental.pallas import tpu as pltpu
from jax.sharding import PartitionSpec as P

MESH = pl.DeviceIdType.MESH
BF16, F32 = jnp.bfloat16, jnp.float32
D, KV, TOK, NZ, NY = 8192, 1024, 256, 4, 4
SHARD = D // NZ
NB = 4
KB = KV // NB
BLK = 512
NBLK = D // BLK
FACTOR = 2.0 ** -7
QR = 208
ORDER = (2, 1, 3, 0)
PR = 1024 - 2 * QR


def kernel(h_ref, gain_ref, codes_ref, scales_ref, cot_ref, pass_ref, ig_ref, wg_ref,
           hv, cv, ct, nv, wall, cod, ng, hp, part, xr, zr, vst, wgv, gv, sv, inv, cdv,
           l_sem, cod_sem, own_sem, h_s, h_r, ct_s, ct_r, z_s, z_r, xw_s, xw_r, sw_s, sw_r,
           xr_s, xr_r, zr_s, zr_r, v_s, v_r, o_sem):
    sec, i, z = lax.axis_index("section"), lax.axis_index("dp"), lax.axis_index("node")
    x, y, c = i // 8, (i // 2) % 4, i % 2

    def dev(xx, yy, zz, cc, ss=None):
        return (sec if ss is None else ss, xx * 8 + yy * 2 + cc, zz)

    zp, zm, z2 = (z + 1) % 4, (z + 3) % 4, (z + 2) % 4
    yp, ym, yo = (y + 1) % 4, (y + 3) % 4, (y + 2) % 4
    d_sib, d_x = dev(x, y, z, 1 - c), dev(1 - x, y, z, c)
    d_y = {(t, k): dev(x, yy, z, c if k == 0 else 1 - c)
           for t, yy in enumerate((yp, ym, yo)) for k in range(2)}
    d_z = [None, dev(x, y, zp, c), dev(x, y, z2, c), dev(x, y, zm, c)]
    d_sec = dev(x, y, z, c, 1 - sec)

    def remote(src, dst, s, r, device):
        return pltpu.make_async_remote_copy(src_ref=src, dst_ref=dst, send_sem=s, recv_sem=r,
                                            device_id=device, device_id_type=MESH)

    def load_h(b):
        return pltpu.make_async_copy(h_ref.at[0, :, pl.ds(pl.multiple_of(b * BLK, BLK), BLK)], hv.at[b], l_sem.at[b])

    def load_codes(kb):
        return pltpu.make_async_copy(codes_ref.at[0, :, pl.ds(kb * KB, KB)], cod.at[kb % 2], cod_sem.at[kb])

    barrier = pltpu.get_barrier_semaphore()
    for target in (d_sib, d_x, *d_y.values(), d_z[1], d_z[2], d_z[3], d_sec):
        pl.semaphore_signal(barrier, inc=1, device_id=target, device_id_type=MESH)

    cp_g = pltpu.make_async_copy(gain_ref, gv, l_sem.at[NBLK])
    cp_s = pltpu.make_async_copy(scales_ref.at[0], sv, l_sem.at[NBLK + 1])
    cp_c = pltpu.make_async_copy(cot_ref.at[0], cv, l_sem.at[NBLK + 2])
    cp_s.start()
    load_codes(0).start()

    @pl.loop(0, NBLK)
    def _(b):
        load_h(b).start()

    cp_c.start()
    load_codes(1).start()
    cp_g.start()

    def h_copy(g, slot):
        xx = (x + 1 + g // 4) % 2
        yy = y if slot < 2 else (yp, ym, yo)[slot // 2 - 1]
        cc = c if slot % 2 == 0 else 1 - c
        lanes = pl.ds(pl.multiple_of(((z + ORDER[g % 4]) % 4) * 128, 128), 128)
        src, dst = hv.at[xx * 8 + yy * 2 + cc, :, lanes], hp.at[g, pl.ds(slot * TOK, TOK)]
        if slot == 0:
            return pltpu.make_async_copy(src, dst, own_sem.at[g])
        return remote(src, dst, h_s.at[g, slot], h_r.at[g, slot],
                      d_sib if slot == 1 else d_y[slot // 2 - 1, slot % 2])

    def h_send(g):
        for slot in (2, 4, 6, 3, 5, 7, 1, 0):
            h_copy(g, slot).start()

    def ct_copy(k):
        def cols(slot):
            return pl.ds(slot * TOK, TOK)

        if k < 3:
            src, dst, target = ct.at[:, cols(0)], ct.at[:, cols((2, 4, 1)[k])], (d_y[0, 0], d_y[1, 0], d_sib)[k]
        elif k < 5:
            rows = pl.ds((k - 3) * (KV // 2), KV // 2)
            src, dst, target = ct.at[rows, cols((2, 4)[k - 3])], ct.at[rows, cols(6)], d_y[k - 3, 0]
        else:
            slot = (2, 4, 6)[k - 5]
            src, dst, target = ct.at[:, cols(slot)], ct.at[:, cols(slot + 1)], d_sib
        return remote(src, dst, ct_s.at[k], ct_r.at[k], target)

    base = c * 1024
    p0 = pl.multiple_of(base + QR, 16)
    q0 = pl.multiple_of(base + x * (QR + PR), 16)
    q1 = pl.multiple_of(base + (1 - x) * (QR + PR), 16)
    r0 = pl.multiple_of(base + x * QR, 16)

    def z_copy(kb, k):
        start, size = (q0, QR) if k < 4 else (p0, PR)
        half = (size + 31) // 32 * 16
        if k % 4 < 2:
            ref = wall.at[kb, z, pl.ds(start, size)]
        elif k % 4 == 2:
            ref = wall.at[kb, zm, pl.ds(start, half)]
        else:
            ref = wall.at[kb, zp, pl.ds(pl.multiple_of(start + half, 16), size - half)]
        return remote(ref, ref, z_s.at[kb, k], z_r.at[kb, k], d_z[1 if k % 2 == 0 else 3])

    shards = (zm, zp, z2)

    def x_copy(kb, k):
        ref = wall.at[kb, shards[k], pl.ds(q0, QR)]
        return remote(ref, ref, xw_s.at[kb, k], xw_r.at[kb, k], d_x)

    def sib_copy(kb, k):
        if k < 3:
            ref = wall.at[kb, shards[k], pl.ds(r0, PR + QR)]
        else:
            ref = wall.at[kb, shards[k - 3], pl.ds(q1, QR)]
        return remote(ref, ref, sw_s.at[kb, k], sw_r.at[kb, k], d_sib)

    def dequant(kb):
        load_codes(kb).wait()

        @pl.loop(0, SHARD // 256)
        def _(g):
            rows = pl.ds(pl.multiple_of(g * 256, 256), 256)
            scale = sv[pl.ds(g, 1), kb * KB:(kb + 1) * KB]
            wall[kb, z, rows, :] = (cod[kb % 2, rows, :].astype(F32) * scale).astype(BF16)

        if kb + 2 < NB:
            load_codes(kb + 2).start()

    def q_send(kb):
        z_copy(kb, 0).start()
        z_copy(kb, 1).start()

    def p_send(kb):
        z_copy(kb, 4).start()
        z_copy(kb, 5).start()

    cp_s.wait()
    dequant(0)

    @pl.loop(0, NBLK)
    def _(b):
        load_h(b).wait()

    pl.semaphore_wait(barrier, 12)
    q_send(0)

    def scale_cot():
        def squares(b, acc):
            v = hv[b].astype(F32)
            v = v * v
            return acc + (v[:, 0:128] + v[:, 128:256]) + (v[:, 256:384] + v[:, 384:512])

        acc = lax.fori_loop(0, NBLK, squares, jnp.zeros((TOK, 128), F32))
        inv[...] = jnp.broadcast_to(lax.rsqrt(jnp.sum(acc, axis=1, keepdims=True) * (1.0 / D) + 1e-05), (TOK, 128))
        cp_c.wait()
        for q in range(4):
            scaled = cv[:, q * 256:(q + 1) * 256].astype(F32) * inv[:, 0:1]
            ct[q * 256:(q + 1) * 256, 0:TOK] = jnp.transpose(scaled).astype(BF16)
        for k in range(3):
            ct_copy(k).start()
        cp_g.wait()

    def ct_first(k):
        ct_copy(k).wait_recv()
        ct_copy(3 + k).start()
        ct_copy(5 + k).start()

    def ct_second():
        ct_copy(3).wait_recv()
        ct_copy(4).wait_recv()
        ct_copy(7).start()
        for k in (2, 5, 6, 7):
            ct_copy(k).wait_recv()

    def xr_copy(g):
        return remote(part.at[g], xr.at[g], xr_s.at[g], xr_r.at[g], d_x)

    def zr_copy(m):
        return remote(part.at[4 + ORDER.index(m)], zr.at[m - 1], zr_s.at[m - 1], zr_r.at[m - 1], d_z[m])

    def grad(g):
        h_copy(g, 0).wait()
        for slot in range(1, 8):
            h_copy(g, slot).wait_recv()
        if g >= 4:
            xr_copy(g - 4).wait_recv()

        @pl.loop(0, 4)
        def _(q):
            rows = pl.ds(pl.multiple_of(q * 256, 256), 256)
            t = jnp.dot(ct[rows, :], hp[g], preferred_element_type=F32) * FACTOR
            if g >= 4:
                t = t + xr[g - 4, rows, :].astype(F32)
            part[g, rows, :] = t.astype(BF16)

        if g < 4:
            xr_copy(g).start()
        elif ORDER[g - 4]:
            zr_copy(ORDER[g - 4]).start()

    d0 = pl.multiple_of(i * 512 + z * 128, 128)

    def grad_last():
        for m in (1, 2, 3):
            zr_copy(m).wait_recv()
        for q in range(4):
            rows = slice(q * 256, (q + 1) * 256)
            total = part[7, rows, :].astype(F32) + zr[0, rows, :].astype(F32)
            total = (total + zr[1, rows, :].astype(F32) + zr[2, rows, :].astype(F32)) * gv[0:1, pl.ds(d0, 128)]
            wgv[:, rows] = jnp.transpose(total).astype(BF16)

    def w_q(kb, k):
        z_copy(kb, k).wait_recv()
        z_copy(kb, 2 + k).start()
        x_copy(kb, k).start()

    def w_p(kb, k):
        z_copy(kb, 4 + k).wait_recv()
        z_copy(kb, 6 + k).start()
        sib_copy(kb, k).start()

    def w_bq(kb):
        z_copy(kb, 2).wait_recv()
        z_copy(kb, 3).wait_recv()
        x_copy(kb, 2).start()

    def w_bp(kb):
        z_copy(kb, 6).wait_recv()
        z_copy(kb, 7).wait_recv()
        sib_copy(kb, 2).start()

    def w_c(kb, k):
        x_copy(kb, k).wait_recv()
        sib_copy(kb, 3 + k).start()

    def pass_copy(kb):
        return remote(vst.at[kb], pass_ref.at[0, :, pl.ds(kb * KB, KB)], v_s.at[kb], v_r.at[kb], d_sec)

    def out_copy(zz):
        return pltpu.make_async_copy(nv.at[zz], ig_ref.at[0, :, pl.ds(pl.multiple_of(zz * SHARD, SHARD), SHARD)],
                                     o_sem.at[zz])

    def h_block(zz, r):
        return hv[zz * 4 + r].astype(F32)

    def gain_block(zz, r):
        return gv[0:1, pl.ds(pl.multiple_of(zz * SHARD + r * BLK, BLK), BLK)]

    def normalize():
        @pl.loop(0, NZ)
        def _(zz):
            for r in range(4):
                nv[zz, :, r * BLK:(r + 1) * BLK] = (h_block(zz, r) * inv[:, 0:1] * gain_block(zz, r)).astype(BF16)

    def grad_of(kb, zz, lo, size):
        return lax.dot_general(cv[:, kb * KB:(kb + 1) * KB], wall[kb, zz, lo:lo + size, :], (((1,), (1,)), ((), ())),
                               preferred_element_type=F32)

    def w_d(kb):
        for k in range(6):
            sib_copy(kb, k).wait_recv()
        cols = slice(kb * KB, (kb + 1) * KB)
        last = kb == NB - 1

        def step(zz, acc):
            if not last:
                for lo in (0, 1024):
                    t = grad_of(kb, zz, lo, 1024)
                    if kb == 0:
                        ng[zz, :, lo:lo + 1024] = t
                    else:
                        ng[zz, :, lo:lo + 1024] = ng[zz, :, lo:lo + 1024] + t
            return acc + jnp.dot(nv[zz], wall[kb, zz], preferred_element_type=F32)

        vals = lax.fori_loop(0, NZ, step, jnp.zeros((TOK, KB), F32))
        vst[kb] = vals.astype(BF16)
        pass_copy(kb).start()
        prod = vals * cv[:, cols].astype(F32)
        prod = prod[:, 0:128] + prod[:, 128:256]
        if kb == 0:
            cdv[...] = prod
        else:
            cdv[...] = cdv[...] + prod

    def w_e():
        kb = NB - 1
        iv = inv[:, 0:1]
        coef = iv * iv * (jnp.sum(cdv[...], axis=1, keepdims=True) * (1.0 / D))

        @pl.loop(0, NZ)
        def _(zz):
            for r in range(4):
                lanes = slice(r * BLK, (r + 1) * BLK)
                t = ng[zz, :, lanes] + grad_of(kb, zz, r * BLK, BLK)
                nv[zz, :, lanes] = (iv * gain_block(zz, r) * t - h_block(zz, r) * coef).astype(BF16)
            out_copy(zz).start()

    h_send(0)
    dequant(1)
    q_send(1)
    dequant(2)
    q_send(2)
    scale_cot()
    h_send(1)
    dequant(3)
    q_send(3)
    w_q(0, 1)
    p_send(0)
    w_q(0, 0)
    normalize()
    w_q(1, 1)
    w_q(1, 0)
    p_send(1)
    w_q(2, 1)
    w_q(2, 0)
    w_c(0, 1)
    w_q(3, 0)
    w_q(3, 1)
    w_c(0, 0)
    w_c(1, 1)
    w_c(1, 0)
    w_p(0, 0)
    ct_first(0)
    ct_first(1)
    w_p(0, 1)
    w_c(2, 1)
    h_send(2)
    w_bq(0)
    h_send(3)
    h_send(4)
    h_send(5)
    w_bq(1)
    h_send(6)
    w_c(2, 0)
    w_c(3, 0)
    w_c(3, 1)
    w_p(1, 0)
    w_p(1, 1)
    w_bq(2)
    p_send(2)
    p_send(3)
    w_c(0, 2)
    w_bq(3)
    h_send(7)
    ct_second()
    w_c(1, 2)
    grad(1)
    w_c(2, 2)
    w_bp(0)
    w_d(0)
    grad(0)
    w_c(3, 2)
    w_bp(1)
    grad(2)
    grad(3)
    w_p(2, 0)
    w_p(2, 1)
    w_d(1)
    w_p(3, 0)
    w_p(3, 1)
    grad(4)
    w_bp(2)
    grad(5)
    w_d(2)
    w_bp(3)
    grad(6)
    w_d(3)
    w_e()
    grad(7)
    grad_last()
    cp_w = pltpu.make_async_copy(wgv, wg_ref.at[0], l_sem.at[NBLK + 3])
    cp_w.start()

    for g in range(8):
        for slot in range(1, 8):
            h_copy(g, slot).wait_send()
    for k in range(8):
        ct_copy(k).wait_send()
    for g in range(4):
        xr_copy(g).wait_send()
    for m in (1, 2, 3):
        zr_copy(m).wait_send()

    for kb in range(NB):
        for k in range(8):
            z_copy(kb, k).wait_send()
        for k in range(3):
            x_copy(kb, k).wait_send()
        for k in range(6):
            sib_copy(kb, k).wait_send()
        pass_copy(kb).wait()

    for zz in range(NZ):
        out_copy(zz).wait()

    cp_w.wait()


def hand_over(a_in, b_in, c_in, a_out, b_out, c_out, a_v, b_v, c_v, sem_in, sem_out):
    refs = [(a_in.at[0], a_v, a_out.at[0]), (c_in.at[0], c_v, c_out.at[0])]
    for k in range(8):
        rows = pl.ds(k * 32, 32)
        refs.append((b_in.at[0, rows], b_v.at[rows], b_out.at[0, rows]))
    first = [pltpu.make_async_copy(a, b, sem_in.at[k]) for k, (a, b, _) in enumerate(refs)]
    second = [pltpu.make_async_copy(b, d, sem_out.at[k]) for k, (_, b, d) in enumerate(refs)]
    for copy in first:
        copy.start()
    for one, two in zip(first, second):
        one.wait()
        two.start()
    for copy in second:
        copy.wait()


def on_device(hidden_in, norm_gain, weight_codes, block_scales, value_grad):
    dma, any_ = pltpu.SemaphoreType.DMA, pl.BlockSpec(memory_space=pl.ANY)
    v = pltpu.VMEM
    out = pl.pallas_call(
        kernel,
        out_shape=(
            jax.ShapeDtypeStruct((1, TOK, KV), BF16),
            jax.ShapeDtypeStruct((1, TOK, D), BF16),
            jax.ShapeDtypeStruct((1, 128, KV), BF16),
        ),
        in_specs=[any_] * 5,
        out_specs=[any_] * 3,
        scratch_shapes=[
            v((NBLK, TOK, BLK), BF16),
            v((TOK, KV), BF16),
            v((KV, 8 * TOK), BF16),
            v((NZ, TOK, SHARD), BF16),
            v((NB, NZ, SHARD, KB), BF16),
            v((2, SHARD, KB), jnp.int32),
            v((NZ, TOK, SHARD), F32),
            v((8, 8 * TOK, 128), BF16),
            v((8, KV, 128), BF16),
            v((4, KV, 128), BF16),
            v((3, KV, 128), BF16),
            v((NB, TOK, KB), BF16),
            v((128, KV), BF16),
            v((1, D), F32),
            v((8, KV), F32),
            v((TOK, 128), F32),
            v((TOK, 128), F32),
            dma((NBLK + 4,)), dma((NB,)),
            dma((8,)), dma((8, 8)), dma((8, 8)), dma((8,)), dma((8,)),
            dma((NB, 8)), dma((NB, 8)), dma((NB, 3)), dma((NB, 3)), dma((NB, 6)), dma((NB, 6)),
            dma((4,)), dma((4,)), dma((3,)), dma((3,)), dma((NB,)), dma((NB,)), dma((NZ,)),
        ],
        compiler_params=pltpu.CompilerParams(
            collective_id=0, has_side_effects=True, vmem_limit_bytes=63 * 2 ** 20),
        cost_estimate=pl.CostEstimate(flops=3 * 2 * TOK * D * KV, bytes_accessed=24 * 2 ** 20, transcendentals=TOK),
    )(hidden_in, norm_gain, weight_codes, block_scales, value_grad)
    return pl.pallas_call(
        hand_over,
        out_shape=tuple(jax.ShapeDtypeStruct(o.shape, o.dtype) for o in out),
        in_specs=[any_] * 3,
        out_specs=[any_] * 3,
        scratch_shapes=[v((TOK, KV), BF16), v((TOK, D), BF16), v((128, KV), BF16), dma((10,)), dma((10,))],
    )(*out)


def solution(mesh):
    return jax.shard_map(
        on_device,
        mesh=mesh,
        in_specs=(
            P("section", ("dp", "node"), None),
            P("section", None),
            P("section", "node", None),
            P("section", "node", None),
            P("section", ("dp", "node"), None),
        ),
        out_specs=(
            P("section", ("dp", "node"), None),
            P("section", ("dp", "node"), None),
            P("section", ("dp", "node"), None),
        ),
        check_vma=False,
    )
```

```python
import functools

import jax
import jax.numpy as jnp
from jax import lax
from jax.experimental import pallas as pl
from jax.experimental.pallas import tpu as pltpu
from jax.sharding import PartitionSpec as P

MESH = pl.DeviceIdType.MESH
BF16, F32 = jnp.bfloat16, jnp.float32
D, KV, TOK, NZ, NY = 8192, 1024, 256, 4, 4
SHARD = D // NZ
NB = 4
KB = KV // NB
BLK = 512
NBLK = D // BLK
FACTOR = 2.0 ** -7
QR = 208
ORDER = (2, 1, 3, 0)
PR = 1024 - 2 * QR


def kernel(h_ref, gain_ref, codes_ref, scales_ref, cot_ref, pass_ref, ig_ref, wg_ref,
           hv, cv, ct, nv, wall, cod, cq, ng, hp, part, xr, zr, zf, vst, gv, sv, inv, cdv,
           hl_sem, l_sem, cod_sem, own_sem, h_r, ct_r, z_r, xw_r, sw_r, xr_r, zr_r, v_r, send_sem):
    sec, i, z = lax.axis_index("section"), lax.axis_index("dp"), lax.axis_index("node")
    x, y, c = i // 8, (i // 2) % 4, i % 2

    def dev(xx, yy, zz, cc, ss=None):
        return (sec if ss is None else ss, xx * 8 + yy * 2 + cc, zz)

    zp, zm, z2 = (z + 1) % 4, (z + 3) % 4, (z + 2) % 4
    yp, ym, yo = (y + 1) % 4, (y + 3) % 4, (y + 2) % 4
    d_sib, d_x = dev(x, y, z, 1 - c), dev(1 - x, y, z, c)
    d_y = {(t, k): dev(x, yy, z, c if k == 0 else 1 - c)
           for t, yy in enumerate((yp, ym, yo)) for k in range(2)}
    d_z = [None, dev(x, y, zp, c), None, dev(x, y, zm, c)]
    d_sec = dev(x, y, z, c, 1 - sec)

    def remote(src, dst, s, r, device):
        return pltpu.make_async_remote_copy(src_ref=src, dst_ref=dst, send_sem=s, recv_sem=r,
                                            device_id=device, device_id_type=MESH)

    def load_h(b):
        return pltpu.make_async_copy(h_ref.at[0, :, pl.ds(pl.multiple_of(b * BLK, BLK), BLK)], hv.at[b], hl_sem.at[0])

    def wait_bytes(ref, sem):
        pltpu.make_async_copy(ref, ref, sem).wait()

    def load_codes(kb):
        return pltpu.make_async_copy(codes_ref.at[0, :, pl.ds(kb * KB, KB)], cod.at[kb % 2], cod_sem.at[kb])

    barrier = pltpu.get_barrier_semaphore()
    for target in (d_sib, d_x, *d_y.values(), d_z[1], d_z[3], d_sec):
        pl.semaphore_signal(barrier, inc=1, device_id=target, device_id_type=MESH)

    cp_g = pltpu.make_async_copy(gain_ref, gv, l_sem.at[0])
    cp_s = pltpu.make_async_copy(scales_ref.at[0], sv, l_sem.at[1])
    cp_c = pltpu.make_async_copy(cot_ref.at[0], cv, l_sem.at[2])
    quick = 4 * c + 3 * x
    cp_q = pltpu.make_async_copy(codes_ref.at[0, pl.ds(pl.multiple_of(quick * 256, 256), 256)], cq, l_sem.at[3])
    cp_q.start()
    cp_s.start()

    @pl.loop(0, NBLK)
    def _(b):
        load_h(b).start()

    cp_c.start()
    load_codes(0).start()
    load_codes(1).start()
    cp_g.start()

    def h_copy(g, slot):
        xx = (x + 1 + g // 4) % 2
        yy = y if slot < 2 else (yp, ym, yo)[slot // 2 - 1]
        cc = c if slot % 2 == 0 else 1 - c
        lanes = pl.ds(pl.multiple_of(((z + ORDER[g % 4]) % 4) * 128, 128), 128)
        src, dst = hv.at[xx * 8 + yy * 2 + cc, :, lanes], hp.at[g, pl.ds(slot * TOK, TOK)]
        if slot == 0:
            return pltpu.make_async_copy(src, dst, own_sem.at[0])
        return remote(src, dst, send_sem.at[0], h_r.at[g],
                      d_sib if slot == 1 else d_y[slot // 2 - 1, slot % 2])

    def h_send(g):
        for slot in (2, 4, 6, 3, 5, 7, 1):
            h_copy(g, slot).start()

    def ct_copy(k):
        def cols(slot):
            return pl.ds(slot * TOK, TOK)

        if k < 3:
            src, dst, target = ct.at[:, cols(0)], ct.at[:, cols((2, 4, 1)[k])], (d_y[0, 0], d_y[1, 0], d_sib)[k]
        elif k < 5:
            rows = pl.ds((k - 3) * (KV // 2), KV // 2)
            src, dst, target = ct.at[rows, cols((2, 4)[k - 3])], ct.at[rows, cols(6)], d_y[k - 3, 0]
        else:
            slot = (2, 4, 6)[k - 5]
            src, dst, target = ct.at[:, cols(slot)], ct.at[:, cols(slot + 1)], d_sib
        return remote(src, dst, send_sem.at[1], ct_r.at[(0, 1, 3, 2, 2, 3, 3, 3)[k]], target)

    base = c * 1024
    p0 = pl.multiple_of(base + QR, 16)
    q0 = pl.multiple_of(base + x * (QR + PR), 16)
    q1 = pl.multiple_of(base + (1 - x) * (QR + PR), 16)
    r0 = pl.multiple_of(base + x * QR, 16)

    def z_copy(kb, k):
        start, size = (q0, QR) if k < 4 else (p0, PR)
        half = (size + 31) // 32 * 16
        if k % 4 < 2:
            ref = wall.at[kb, z, pl.ds(start, size)]
        elif k % 4 == 2:
            ref = wall.at[kb, zm, pl.ds(start, half)]
        else:
            ref = wall.at[kb, zp, pl.ds(pl.multiple_of(start + half, 16), size - half)]
        return remote(ref, ref, send_sem.at[2], z_r.at[kb, (0, 1, 2, 2, 3, 4, 5, 5)[k]], d_z[1 if k % 2 == 0 else 3])

    shards = (zm, zp, z2)

    def x_copy(kb, k):
        ref = wall.at[kb, shards[k], pl.ds(q0, QR)]
        return remote(ref, ref, send_sem.at[3], xw_r.at[kb], d_x)

    def sib_copy(kb, k):
        if k < 3:
            ref = wall.at[kb, shards[k], pl.ds(r0, PR + QR)]
        else:
            ref = wall.at[kb, shards[k - 3], pl.ds(q1, QR)]
        return remote(ref, ref, send_sem.at[4], sw_r.at[kb], d_sib)

    def dequant(kb):
        load_codes(kb).wait()

        @pl.loop(1, SHARD // 256)
        def _(t):
            g = (quick + t) % (SHARD // 256)
            rows = pl.ds(pl.multiple_of(g * 256, 256), 256)
            scale = sv[pl.ds(g, 1), kb * KB:(kb + 1) * KB]
            wall[kb, z, rows, :] = (cod[kb % 2, rows, :].astype(F32) * scale).astype(BF16)

        if kb + 2 < NB:
            load_codes(kb + 2).start()

    def p_send(kb):
        z_copy(kb, 4).start()
        z_copy(kb, 5).start()

    cp_q.wait()
    cp_s.wait()
    for kb in range(NB):
        cols = slice(kb * KB, (kb + 1) * KB)
        wall[kb, z, pl.ds(pl.multiple_of(quick * 256, 256), 256), :] = (
            cq[:, cols].astype(F32) * sv[pl.ds(quick, 1), cols]).astype(BF16)
    pl.semaphore_wait(barrier, 11)
    for kb in range(NB):
        z_copy(kb, 0).start()
        z_copy(kb, 1).start()
    wait_bytes(hv, hl_sem.at[0])

    def scale_cot():
        def squares(b, acc):
            v = hv[b].astype(F32)
            v = v * v
            return acc + (v[:, 0:128] + v[:, 128:256]) + (v[:, 256:384] + v[:, 384:512])

        acc = lax.fori_loop(0, NBLK, squares, jnp.zeros((TOK, 128), F32))
        inv[...] = jnp.broadcast_to(lax.rsqrt(jnp.sum(acc, axis=1, keepdims=True) * (1.0 / D) + 1e-05), (TOK, 128))
        cp_c.wait()
        for q in range(4):
            scaled = cv[:, q * 256:(q + 1) * 256].astype(F32) * inv[:, 0:1]
            ct[q * 256:(q + 1) * 256, 0:TOK] = jnp.transpose(scaled).astype(BF16)
        for k in range(3):
            ct_copy(k).start()
        cp_g.wait()
        for g in range(8):
            h_copy(g, 0).start()

    def ct_first(k):
        ct_copy(k).wait_recv()
        ct_copy(3 + k).start()
        ct_copy(5 + k).start()

    def ct_second():
        wait_bytes(ct.at[:, pl.ds(0, TOK)], ct_r.at[2])
        ct_copy(7).start()
        wait_bytes(ct.at[:, pl.ds(0, 4 * TOK)], ct_r.at[3])
        wait_bytes(hp.at[:, pl.ds(0, TOK)], own_sem.at[0])

    def xr_copy(g):
        return remote(part.at[g], xr.at[g], send_sem.at[5], xr_r.at[g], d_x)

    def zr_copy(m):
        up = m % 2 == 0
        if m < 2:
            return remote(part.at[5 + m], zr.at[m], send_sem.at[6], zr_r.at[m], d_z[1 if up else 3])
        rows = pl.ds((m - 2) * (KV // 2), KV // 2)
        return remote(part.at[4, rows], zf.at[m - 2], send_sem.at[6], zr_r.at[m], d_z[1 if up else 3])

    def grad(g):
        wait_bytes(hp.at[g, pl.ds(TOK, 7 * TOK)], h_r.at[g])
        if g >= 4:
            xr_copy(g - 4).wait_recv()
        if g in (5, 6):
            zr_copy(g - 3).wait_recv()
        for q in range(4):
            rows = slice(q * 256, (q + 1) * 256)
            t = jnp.dot(ct[rows, :], hp[g], preferred_element_type=F32) * FACTOR
            if g >= 4:
                t = t + xr[g - 4, rows, :].astype(F32)
            if g in (5, 6) and q // 2 == g - 5:
                t = t + zf[g - 5, (q % 2) * 256:(q % 2 + 1) * 256, :].astype(F32)
            part[g, rows, :] = t.astype(BF16)
        if g < 4:
            xr_copy(g).start()
        elif g == 4:
            zr_copy(2).start()
            zr_copy(3).start()
        elif g < 7:
            zr_copy(g - 5).start()

    d0 = pl.multiple_of(i * 512 + z * 128, 128)

    def grad_last():
        zr_copy(0).wait_recv()
        zr_copy(1).wait_recv()
        for q in range(4):
            rows = slice(q * 256, (q + 1) * 256)
            total = part[7, rows, :].astype(F32) + zr[0, rows, :].astype(F32) + zr[1, rows, :].astype(F32)
            total = total * gv[0:1, pl.ds(d0, 128)]
            wg_ref[0, :, rows] = jnp.transpose(total).astype(BF16)

    def w_q(kb, k):
        z_copy(kb, k).wait_recv()
        z_copy(kb, 2 + k).start()
        x_copy(kb, k).start()

    def w_p(kb, k):
        z_copy(kb, 4 + k).wait_recv()
        z_copy(kb, 6 + k).start()
        sib_copy(kb, k).start()

    def w_bq(kb):
        wait_bytes(wall.at[kb, 0, pl.ds(0, QR)], z_r.at[kb, 2])
        x_copy(kb, 2).start()

    def w_bp(kb):
        wait_bytes(wall.at[kb, 0, pl.ds(0, PR)], z_r.at[kb, 5])
        sib_copy(kb, 2).start()

    def w_c(kb):
        wait_bytes(wall.at[kb, pl.ds(0, 3), pl.ds(0, QR)], xw_r.at[kb])
        for k in range(3):
            sib_copy(kb, 3 + k).start()

    def pass_copy(kb):
        return remote(vst.at[kb], pass_ref.at[0, :, pl.ds(kb * KB, KB)], send_sem.at[7], v_r.at[0], d_sec)

    def h_block(zz, r):
        return hv[zz * 4 + r].astype(F32)

    def gain_block(zz, r):
        return gv[0:1, pl.ds(pl.multiple_of(zz * SHARD + r * BLK, BLK), BLK)]

    def normalize():
        @pl.loop(0, NZ)
        def _(zz):
            for r in range(4):
                nv[zz, :, r * BLK:(r + 1) * BLK] = (h_block(zz, r) * inv[:, 0:1] * gain_block(zz, r)).astype(BF16)

    def grad_of(kb, zz, lo, size):
        return lax.dot_general(cv[:, kb * KB:(kb + 1) * KB], wall[kb, zz, lo:lo + size, :], (((1,), (1,)), ((), ())),
                               preferred_element_type=F32)

    def w_d(kb):
        wait_bytes(wall.at[kb, pl.ds(0, 3), pl.ds(0, 1024)], sw_r.at[kb])
        cols = slice(kb * KB, (kb + 1) * KB)
        last = kb == NB - 1

        def step(zz, acc):
            if not last:
                for lo in (0, 1024):
                    t = grad_of(kb, zz, lo, 1024)
                    if kb == 0:
                        ng[zz, :, lo:lo + 1024] = t
                    else:
                        ng[zz, :, lo:lo + 1024] = ng[zz, :, lo:lo + 1024] + t
            return acc + jnp.dot(nv[zz], wall[kb, zz], preferred_element_type=F32)

        vals = lax.fori_loop(0, NZ, step, jnp.zeros((TOK, KB), F32))
        vst[kb] = vals.astype(BF16)
        pass_copy(kb).start()
        prod = vals * cv[:, cols].astype(F32)
        prod = prod[:, 0:128] + prod[:, 128:256]
        if kb == 0:
            cdv[...] = prod
        else:
            cdv[...] = cdv[...] + prod

    def w_e():
        kb = NB - 1
        iv = inv[:, 0:1]
        coef = iv * iv * (jnp.sum(cdv[...], axis=1, keepdims=True) * (1.0 / D))

        @pl.loop(0, NZ)
        def _(zz):
            for r in range(4):
                lanes = slice(r * BLK, (r + 1) * BLK)
                t = ng[zz, :, lanes] + grad_of(kb, zz, r * BLK, BLK)
                ig_ref[0, :, pl.ds(pl.multiple_of(zz * SHARD + r * BLK, BLK), BLK)] = (
                    iv * gain_block(zz, r) * t - h_block(zz, r) * coef).astype(BF16)

    h_send(0)
    scale_cot()
    h_send(1)
    dequant(0)
    dequant(1)
    dequant(2)
    p_send(0)
    w_q(0, 0)
    w_q(0, 1)
    normalize()
    w_q(1, 0)
    w_q(1, 1)
    w_q(2, 0)
    w_q(2, 1)
    w_q(3, 0)
    w_q(3, 1)
    dequant(3)
    w_p(0, 0)
    w_p(0, 1)
    w_bq(0)
    ct_first(0)
    ct_first(1)
    w_bq(1)
    p_send(1)
    h_send(2)
    h_send(3)
    p_send(2)
    h_send(4)
    w_bq(2)
    h_send(5)
    h_send(6)
    h_send(7)
    w_bq(3)
    w_bp(0)
    w_c(0)
    w_d(0)
    ct_second()
    w_p(1, 0)
    w_p(1, 1)
    w_c(1)
    w_c(2)
    grad(0)
    grad(1)
    grad(2)
    w_p(2, 0)
    w_p(2, 1)
    w_c(3)
    p_send(3)
    w_bp(1)
    grad(3)
    w_d(1)
    w_bp(2)
    grad(4)
    w_d(2)
    w_p(3, 0)
    w_p(3, 1)
    grad(5)
    w_bp(3)
    grad(6)
    w_d(3)
    w_e()
    grad(7)
    grad_last()
    wait_bytes(pass_ref, v_r.at[0])
    wait_bytes(hp.at[:, pl.ds(0, 7 * TOK)], send_sem.at[0])
    wait_bytes(ct.at[:, pl.ds(0, 7 * TOK)], send_sem.at[1])
    wait_bytes(wall.at[:, pl.ds(0, 3), pl.ds(0, PR + QR)], send_sem.at[2])
    wait_bytes(wall.at[:, pl.ds(0, 3), pl.ds(0, QR)], send_sem.at[3])
    wait_bytes(wall.at[:, pl.ds(0, 3), pl.ds(0, 1024)], send_sem.at[4])
    wait_bytes(part.at[pl.ds(0, 4)], send_sem.at[5])
    wait_bytes(part.at[pl.ds(4, 3)], send_sem.at[6])
    wait_bytes(vst, send_sem.at[7])


def hand_over(a_in, b_in, c_in, a_out, b_out, c_out, sem):
    copies = [pltpu.make_async_copy(a_in, a_out, sem.at[0]), pltpu.make_async_copy(c_in, c_out, sem.at[1])]
    for k in range(8):
        rows = pl.ds(k * 32, 32)
        copies.append(pltpu.make_async_copy(b_in.at[0, rows], b_out.at[0, rows], sem.at[2 + k]))
    for copy in copies:
        copy.start()
    for copy in copies:
        copy.wait()


def on_device(hidden_in, norm_gain, weight_codes, block_scales, value_grad):
    dma, any_ = pltpu.SemaphoreType.DMA, pl.BlockSpec(memory_space=pl.ANY)
    v = pltpu.VMEM
    out = pl.pallas_call(
        kernel,
        out_shape=(v((1, TOK, KV), BF16), v((1, TOK, D), BF16), v((1, 128, KV), BF16)),
        in_specs=[any_] * 5,
        out_specs=[pl.BlockSpec(memory_space=v)] * 3,
        scratch_shapes=[
            v((NBLK, TOK, BLK), BF16),
            v((TOK, KV), BF16),
            v((KV, 8 * TOK), BF16),
            v((NZ, TOK, SHARD), BF16),
            v((NB, NZ, SHARD, KB), BF16),
            v((2, SHARD, KB), jnp.int32),
            v((256, KV), jnp.int32),
            v((NZ, TOK, SHARD), F32),
            v((8, 8 * TOK, 128), BF16),
            v((8, KV, 128), BF16),
            v((4, KV, 128), BF16),
            v((2, KV, 128), BF16),
            v((2, KV // 2, 128), BF16),
            v((NB, TOK, KB), BF16),
            v((1, D), F32),
            v((8, KV), F32),
            v((TOK, 128), F32),
            v((TOK, 128), F32),
            dma((1,)), dma((4,)), dma((NB,)), dma((1,)), dma((8,)), dma((4,)), dma((NB, 6)), dma((NB,)), dma((NB,)),
            dma((4,)), dma((4,)), dma((1,)), dma((8,)),
        ],
        compiler_params=pltpu.CompilerParams(
            collective_id=0, has_side_effects=True, vmem_limit_bytes=57 * 2 ** 20),
        cost_estimate=pl.CostEstimate(flops=3 * 2 * TOK * D * KV, bytes_accessed=24 * 2 ** 20, transcendentals=TOK),
    )(hidden_in, norm_gain, weight_codes, block_scales, value_grad)
    return pl.pallas_call(
        hand_over,
        out_shape=tuple(jax.ShapeDtypeStruct(o.shape, o.dtype) for o in out),
        in_specs=[pl.BlockSpec(memory_space=v)] * 3,
        out_specs=[any_] * 3,
        scratch_shapes=[dma((10,))],
        compiler_params=pltpu.CompilerParams(vmem_limit_bytes=2 * 2 ** 20),
    )(*out)


def solution(mesh):
    return jax.shard_map(
        on_device,
        mesh=mesh,
        in_specs=(
            P("section", ("dp", "node"), None),
            P("section", None),
            P("section", "node", None),
            P("section", "node", None),
            P("section", ("dp", "node"), None),
        ),
        out_specs=(
            P("section", ("dp", "node"), None),
            P("section", ("dp", "node"), None),
            P("section", ("dp", "node"), None),
        ),
        check_vma=False,
    )
```

```python
import functools

import jax
import jax.numpy as jnp
from jax import lax
from jax.experimental import pallas as pl
from jax.experimental.pallas import tpu as pltpu
from jax.sharding import PartitionSpec as P

MESH = pl.DeviceIdType.MESH
BF16, F32 = jnp.bfloat16, jnp.float32
D, KV, TOK, NZ, NY = 8192, 1024, 256, 4, 4
SHARD = D // NZ
NB = 4
KB = KV // NB
BLK = 512
NBLK = D // BLK
FACTOR = 2.0 ** -7
QR = 208
ORDER = (2, 1, 3, 0)
PR = 1024 - 2 * QR


def kernel(h_ref, gain_ref, codes_ref, scales_ref, cot_ref, pass_ref, ig_ref, wg_ref,
           hv, cv, ct, nv, wall, cod, cq, ng, hp, part, xr, zr, zf, vst, gv, sv, inv, cdv,
           hl_sem, l_sem, cod_sem, own_sem, h_r, ct_r, z_r, xw_r, sw_r, xr_r, zr_r, v_r, send_sem):
    sec, i, z = lax.axis_index("section"), lax.axis_index("dp"), lax.axis_index("node")
    x, y, c = i // 8, (i // 2) % 4, i % 2

    def dev(xx, yy, zz, cc, ss=None):
        return (sec if ss is None else ss, xx * 8 + yy * 2 + cc, zz)

    zp, zm, z2 = (z + 1) % 4, (z + 3) % 4, (z + 2) % 4
    yp, ym, yo = (y + 1) % 4, (y + 3) % 4, (y + 2) % 4
    d_sib, d_x = dev(x, y, z, 1 - c), dev(1 - x, y, z, c)
    d_y = {(t, k): dev(x, yy, z, c if k == 0 else 1 - c)
           for t, yy in enumerate((yp, ym, yo)) for k in range(2)}
    d_z = [None, dev(x, y, zp, c), None, dev(x, y, zm, c)]
    d_sec = dev(x, y, z, c, 1 - sec)

    def remote(src, dst, s, r, device):
        return pltpu.make_async_remote_copy(src_ref=src, dst_ref=dst, send_sem=s, recv_sem=r,
                                            device_id=device, device_id_type=MESH)

    def load_h(b):
        return pltpu.make_async_copy(h_ref.at[0, :, pl.ds(pl.multiple_of(b * BLK, BLK), BLK)], hv.at[b], hl_sem.at[0])

    def wait_bytes(ref, sem):
        pltpu.make_async_copy(ref, ref, sem).wait()

    def load_codes(kb):
        return pltpu.make_async_copy(codes_ref.at[0, :, pl.ds(kb * KB, KB)], cod.at[kb % 2], cod_sem.at[kb])

    barrier = pltpu.get_barrier_semaphore()
    for target in (d_sib, d_x, *d_y.values(), d_z[1], d_z[3], d_sec):
        pl.semaphore_signal(barrier, inc=1, device_id=target, device_id_type=MESH)

    cp_g = pltpu.make_async_copy(gain_ref, gv, l_sem.at[0])
    cp_s = pltpu.make_async_copy(scales_ref.at[0], sv, l_sem.at[1])
    cp_c = pltpu.make_async_copy(cot_ref.at[0], cv, l_sem.at[2])
    quick = 4 * c + 3 * x
    cp_q = pltpu.make_async_copy(codes_ref.at[0, pl.ds(pl.multiple_of(quick * 256, 256), 256)], cq, l_sem.at[3])
    cp_q.start()
    cp_s.start()

    @pl.loop(0, NBLK)
    def _(b):
        load_h(b).start()

    cp_c.start()
    load_codes(0).start()
    load_codes(1).start()
    cp_g.start()

    def h_copy(g, slot):
        xx = (x + 1 + g // 4) % 2
        yy = y if slot < 2 else (yp, ym, yo)[slot // 2 - 1]
        cc = c if slot % 2 == 0 else 1 - c
        lanes = pl.ds(pl.multiple_of(((z + ORDER[g % 4]) % 4) * 128, 128), 128)
        b = xx * 8 + yy * 2 + cc
        src, dst = hv.at[b, :, lanes], hp.at[g, pl.ds(slot * TOK, TOK)]
        if g == 0 and slot:
            col = b * BLK + ((z + ORDER[0]) % 4) * 128
            src = h_ref.at[0, :, pl.ds(pl.multiple_of(col, 128), 128)]
        if slot == 0:
            return pltpu.make_async_copy(src, dst, own_sem.at[0])
        return remote(src, dst, send_sem.at[0], h_r.at[g],
                      d_sib if slot == 1 else d_y[slot // 2 - 1, slot % 2])

    def h_send(g):
        for slot in (2, 4, 6, 3, 5, 7, 1):
            h_copy(g, slot).start()

    def ct_copy(k):
        def cols(slot):
            return pl.ds(slot * TOK, TOK)

        if k < 3:
            src, dst, target = ct.at[:, cols(0)], ct.at[:, cols((2, 4, 1)[k])], (d_y[0, 0], d_y[1, 0], d_sib)[k]
        elif k < 5:
            rows = pl.ds((k - 3) * (KV // 2), KV // 2)
            src, dst, target = ct.at[rows, cols((2, 4)[k - 3])], ct.at[rows, cols(6)], d_y[k - 3, 0]
        else:
            slot = (2, 4, 6)[k - 5]
            src, dst, target = ct.at[:, cols(slot)], ct.at[:, cols(slot + 1)], d_sib
        return remote(src, dst, send_sem.at[1], ct_r.at[(0, 1, 3, 2, 2, 3, 3, 3)[k]], target)

    base = c * 1024
    p0 = pl.multiple_of(base + QR, 16)
    q0 = pl.multiple_of(base + x * (QR + PR), 16)
    q1 = pl.multiple_of(base + (1 - x) * (QR + PR), 16)
    r0 = pl.multiple_of(base + x * QR, 16)

    def z_copy(kb, k):
        start, size = (q0, QR) if k < 4 else (p0, PR)
        half = (size + 31) // 32 * 16
        if k % 4 < 2:
            ref = wall.at[kb, z, pl.ds(start, size)]
        elif k % 4 == 2:
            ref = wall.at[kb, zm, pl.ds(start, half)]
        else:
            ref = wall.at[kb, zp, pl.ds(pl.multiple_of(start + half, 16), size - half)]
        return remote(ref, ref, send_sem.at[2], z_r.at[kb, (0, 1, 2, 2, 3, 4, 5, 5)[k]], d_z[1 if k % 2 == 0 else 3])

    shards = (zm, zp, z2)

    def x_copy(kb, k):
        ref = wall.at[kb, shards[k], pl.ds(q0, QR)]
        return remote(ref, ref, send_sem.at[3], xw_r.at[kb], d_x)

    def sib_copy(kb, k):
        if k < 3:
            ref = wall.at[kb, shards[k], pl.ds(r0, PR + QR)]
        else:
            ref = wall.at[kb, shards[k - 3], pl.ds(q1, QR)]
        return remote(ref, ref, send_sem.at[4], sw_r.at[kb], d_sib)

    def dequant(kb):
        load_codes(kb).wait()

        @pl.loop(1, SHARD // 256)
        def _(t):
            g = (quick + t) % (SHARD // 256)
            rows = pl.ds(pl.multiple_of(g * 256, 256), 256)
            scale = sv[pl.ds(g, 1), kb * KB:(kb + 1) * KB]
            wall[kb, z, rows, :] = (cod[kb % 2, rows, :].astype(F32) * scale).astype(BF16)

        if kb + 2 < NB:
            load_codes(kb + 2).start()

    def p_send(kb):
        z_copy(kb, 4).start()
        z_copy(kb, 5).start()

    pl.semaphore_wait(barrier, 11)
    h_send(0)
    cp_q.wait()
    cp_s.wait()
    for kb in range(NB):
        cols = slice(kb * KB, (kb + 1) * KB)
        wall[kb, z, pl.ds(pl.multiple_of(quick * 256, 256), 256), :] = (
            cq[:, cols].astype(F32) * sv[pl.ds(quick, 1), cols]).astype(BF16)
        z_copy(kb, 0).start()
        z_copy(kb, 1).start()

    def scale_cot():
        wait_bytes(hv, hl_sem.at[0])

        def squares(b, acc):
            v = hv[b].astype(F32)
            v = v * v
            return acc + (v[:, 0:128] + v[:, 128:256]) + (v[:, 256:384] + v[:, 384:512])

        acc = lax.fori_loop(0, NBLK, squares, jnp.zeros((TOK, 128), F32))
        inv[...] = jnp.broadcast_to(lax.rsqrt(jnp.sum(acc, axis=1, keepdims=True) * (1.0 / D) + 1e-05), (TOK, 128))
        cp_c.wait()
        for q in range(4):
            scaled = cv[:, q * 256:(q + 1) * 256].astype(F32) * inv[:, 0:1]
            ct[q * 256:(q + 1) * 256, 0:TOK] = jnp.transpose(scaled).astype(BF16)
        for k in range(3):
            ct_copy(k).start()
        cp_g.wait()
        for g in range(8):
            h_copy(g, 0).start()

    def ct_first(k):
        ct_copy(k).wait_recv()
        ct_copy(3 + k).start()
        ct_copy(5 + k).start()

    def ct_second():
        wait_bytes(ct.at[:, pl.ds(0, TOK)], ct_r.at[2])
        ct_copy(7).start()
        wait_bytes(ct.at[:, pl.ds(0, 4 * TOK)], ct_r.at[3])
        wait_bytes(hp.at[:, pl.ds(0, TOK)], own_sem.at[0])

    def xr_copy(g):
        return remote(part.at[g], xr.at[g], send_sem.at[5], xr_r.at[g], d_x)

    def zr_copy(m, half=0):
        up = m % 2 == 0
        if m < 2:
            rows = pl.ds(half * (KV // 2), KV // 2)
            return remote(part.at[5 + m, rows], zr.at[m, rows], send_sem.at[6], zr_r.at[m], d_z[1 if up else 3])
        rows = pl.ds((m - 2) * (KV // 2), KV // 2)
        return remote(part.at[4, rows], zf.at[m - 2], send_sem.at[6], zr_r.at[m], d_z[1 if up else 3])

    def grad(g):
        wait_bytes(hp.at[g, pl.ds(TOK, 7 * TOK)], h_r.at[g])
        if g >= 4:
            xr_copy(g - 4).wait_recv()
        if g in (5, 6):
            zr_copy(g - 3).wait_recv()
        for q in range(4):
            rows = slice(q * 256, (q + 1) * 256)
            t = jnp.dot(ct[rows, :], hp[g], preferred_element_type=F32) * FACTOR
            if g >= 4:
                t = t + xr[g - 4, rows, :].astype(F32)
            if g in (5, 6) and q // 2 == g - 5:
                t = t + zf[g - 5, (q % 2) * 256:(q % 2 + 1) * 256, :].astype(F32)
            part[g, rows, :] = t.astype(BF16)
            if g in (5, 6) and q % 2:
                zr_copy(g - 5, q // 2).start()
        if g < 4:
            xr_copy(g).start()
        elif g == 4:
            zr_copy(2).start()
            zr_copy(3).start()

    d0 = pl.multiple_of(i * 512 + z * 128, 128)

    def grad_last():
        wait_bytes(zr.at[0], zr_r.at[0])
        wait_bytes(zr.at[1], zr_r.at[1])
        for q in range(4):
            rows = slice(q * 256, (q + 1) * 256)
            total = part[7, rows, :].astype(F32) + zr[0, rows, :].astype(F32) + zr[1, rows, :].astype(F32)
            total = total * gv[0:1, pl.ds(d0, 128)]
            wg_ref[0, :, rows] = jnp.transpose(total).astype(BF16)

    def w_q(kb, k):
        z_copy(kb, k).wait_recv()
        z_copy(kb, 2 + k).start()
        x_copy(kb, k).start()

    def w_p(kb, k):
        z_copy(kb, 4 + k).wait_recv()
        z_copy(kb, 6 + k).start()
        sib_copy(kb, k).start()

    def w_bq(kb):
        wait_bytes(wall.at[kb, 0, pl.ds(0, QR)], z_r.at[kb, 2])
        x_copy(kb, 2).start()

    def w_bp(kb):
        wait_bytes(wall.at[kb, 0, pl.ds(0, PR)], z_r.at[kb, 5])
        sib_copy(kb, 2).start()

    def w_c(kb):
        wait_bytes(wall.at[kb, pl.ds(0, 3), pl.ds(0, QR)], xw_r.at[kb])
        for k in range(3):
            sib_copy(kb, 3 + k).start()

    def pass_copy(kb):
        return remote(vst.at[kb], pass_ref.at[0, :, pl.ds(kb * KB, KB)], send_sem.at[7], v_r.at[0], d_sec)

    def h_block(zz, r):
        return hv[zz * 4 + r].astype(F32)

    def gain_block(zz, r):
        return gv[0:1, pl.ds(pl.multiple_of(zz * SHARD + r * BLK, BLK), BLK)]

    def normalize():
        @pl.loop(0, NZ)
        def _(zz):
            for r in range(4):
                nv[zz, :, r * BLK:(r + 1) * BLK] = (h_block(zz, r) * inv[:, 0:1] * gain_block(zz, r)).astype(BF16)

    def grad_of(kb, zz, lo, size):
        return lax.dot_general(cv[:, kb * KB:(kb + 1) * KB], wall[kb, zz, lo:lo + size, :], (((1,), (1,)), ((), ())),
                               preferred_element_type=F32)

    def w_d(kb):
        wait_bytes(wall.at[kb, pl.ds(0, 3), pl.ds(0, 1024)], sw_r.at[kb])
        cols = slice(kb * KB, (kb + 1) * KB)
        last = kb == NB - 1

        def step(zz, acc):
            if not last:
                for lo in (0, 1024):
                    t = grad_of(kb, zz, lo, 1024)
                    if kb == 0:
                        ng[zz, :, lo:lo + 1024] = t
                    else:
                        ng[zz, :, lo:lo + 1024] = ng[zz, :, lo:lo + 1024] + t
            return acc + jnp.dot(nv[zz], wall[kb, zz], preferred_element_type=F32)

        vals = lax.fori_loop(0, NZ, step, jnp.zeros((TOK, KB), F32))
        vst[kb] = vals.astype(BF16)
        pass_copy(kb).start()
        prod = vals * cv[:, cols].astype(F32)
        prod = prod[:, 0:128] + prod[:, 128:256]
        if kb == 0:
            cdv[...] = prod
        else:
            cdv[...] = cdv[...] + prod

    def w_e():
        kb = NB - 1
        iv = inv[:, 0:1]
        coef = iv * iv * (jnp.sum(cdv[...], axis=1, keepdims=True) * (1.0 / D))

        @pl.loop(0, NZ)
        def _(zz):
            for r in range(4):
                lanes = slice(r * BLK, (r + 1) * BLK)
                t = ng[zz, :, lanes] + grad_of(kb, zz, r * BLK, BLK)
                ig_ref[0, :, pl.ds(pl.multiple_of(zz * SHARD + r * BLK, BLK), BLK)] = (
                    iv * gain_block(zz, r) * t - h_block(zz, r) * coef).astype(BF16)

    scale_cot()
    h_send(1)
    dequant(0)
    w_q(0, 0)
    w_q(0, 1)
    p_send(0)
    normalize()
    w_q(1, 1)
    w_q(1, 0)
    w_q(2, 1)
    w_q(2, 0)
    w_q(3, 1)
    dequant(1)
    dequant(2)
    dequant(3)
    w_bq(0)
    w_q(3, 0)
    ct_first(0)
    ct_first(1)
    h_send(2)
    w_p(0, 0)
    w_p(0, 1)
    w_bq(1)
    h_send(3)
    h_send(4)
    h_send(5)
    h_send(6)
    w_bq(2)
    w_bq(3)
    p_send(1)
    p_send(2)
    w_c(0)
    w_bp(0)
    w_d(0)
    ct_second()
    w_c(1)
    w_c(2)
    w_p(1, 1)
    grad(0)
    w_c(3)
    w_p(1, 0)
    grad(1)
    grad(2)
    w_p(2, 0)
    w_p(2, 1)
    h_send(7)
    grad(3)
    w_bp(1)
    p_send(3)
    w_d(1)
    w_bp(2)
    grad(4)
    w_d(2)
    w_p(3, 0)
    w_p(3, 1)
    grad(5)
    grad(6)
    w_bp(3)
    w_d(3)
    w_e()
    grad(7)
    grad_last()
    wait_bytes(pass_ref, v_r.at[0])
    wait_bytes(hp.at[:, pl.ds(0, 7 * TOK)], send_sem.at[0])
    wait_bytes(ct.at[:, pl.ds(0, 7 * TOK)], send_sem.at[1])
    wait_bytes(wall.at[:, pl.ds(0, 3), pl.ds(0, PR + QR)], send_sem.at[2])
    wait_bytes(wall.at[:, pl.ds(0, 3), pl.ds(0, QR)], send_sem.at[3])
    wait_bytes(wall.at[:, pl.ds(0, 3), pl.ds(0, 1024)], send_sem.at[4])
    wait_bytes(part.at[pl.ds(0, 4)], send_sem.at[5])
    wait_bytes(part.at[pl.ds(4, 3)], send_sem.at[6])
    wait_bytes(vst, send_sem.at[7])


def hand_over(a_in, b_in, c_in, a_out, b_out, c_out, sem):
    copies = [pltpu.make_async_copy(a_in, a_out, sem.at[0]), pltpu.make_async_copy(c_in, c_out, sem.at[1])]
    for k in range(8):
        rows = pl.ds(k * 32, 32)
        copies.append(pltpu.make_async_copy(b_in.at[0, rows], b_out.at[0, rows], sem.at[2 + k]))
    for copy in copies:
        copy.start()
    for copy in copies:
        copy.wait()


def on_device(hidden_in, norm_gain, weight_codes, block_scales, value_grad):
    dma, any_ = pltpu.SemaphoreType.DMA, pl.BlockSpec(memory_space=pl.ANY)
    v = pltpu.VMEM
    out = pl.pallas_call(
        kernel,
        out_shape=(v((1, TOK, KV), BF16), v((1, TOK, D), BF16), v((1, 128, KV), BF16)),
        in_specs=[any_] * 5,
        out_specs=[pl.BlockSpec(memory_space=v)] * 3,
        scratch_shapes=[
            v((NBLK, TOK, BLK), BF16),
            v((TOK, KV), BF16),
            v((KV, 8 * TOK), BF16),
            v((NZ, TOK, SHARD), BF16),
            v((NB, NZ, SHARD, KB), BF16),
            v((2, SHARD, KB), jnp.int32),
            v((256, KV), jnp.int32),
            v((NZ, TOK, SHARD), F32),
            v((8, 8 * TOK, 128), BF16),
            v((8, KV, 128), BF16),
            v((4, KV, 128), BF16),
            v((2, KV, 128), BF16),
            v((2, KV // 2, 128), BF16),
            v((NB, TOK, KB), BF16),
            v((1, D), F32),
            v((8, KV), F32),
            v((TOK, 128), F32),
            v((TOK, 128), F32),
            dma((1,)), dma((4,)), dma((NB,)), dma((1,)), dma((8,)), dma((4,)), dma((NB, 6)), dma((NB,)), dma((NB,)),
            dma((4,)), dma((4,)), dma((1,)), dma((8,)),
        ],
        compiler_params=pltpu.CompilerParams(
            collective_id=0, has_side_effects=True, vmem_limit_bytes=57 * 2 ** 20),
        cost_estimate=pl.CostEstimate(flops=3 * 2 * TOK * D * KV, bytes_accessed=24 * 2 ** 20, transcendentals=TOK),
    )(hidden_in, norm_gain, weight_codes, block_scales, value_grad)
    return pl.pallas_call(
        hand_over,
        out_shape=tuple(jax.ShapeDtypeStruct(o.shape, o.dtype) for o in out),
        in_specs=[pl.BlockSpec(memory_space=v)] * 3,
        out_specs=[any_] * 3,
        scratch_shapes=[dma((10,))],
        compiler_params=pltpu.CompilerParams(vmem_limit_bytes=2 * 2 ** 20),
    )(*out)


def solution(mesh):
    return jax.shard_map(
        on_device,
        mesh=mesh,
        in_specs=(
            P("section", ("dp", "node"), None),
            P("section", None),
            P("section", "node", None),
            P("section", "node", None),
            P("section", ("dp", "node"), None),
        ),
        out_specs=(
            P("section", ("dp", "node"), None),
            P("section", ("dp", "node"), None),
            P("section", ("dp", "node"), None),
        ),
        check_vma=False,
    )
```

```python
import functools

import jax
import jax.numpy as jnp
from jax import lax
from jax.experimental import pallas as pl
from jax.experimental.pallas import tpu as pltpu
from jax.sharding import PartitionSpec as P

MESH = pl.DeviceIdType.MESH
BF16, F32 = jnp.bfloat16, jnp.float32
D, KV, TOK, NZ, NY = 8192, 1024, 256, 4, 4
SHARD = D // NZ
NB = 4
KB = KV // NB
BLK = 512
NBLK = D // BLK
FACTOR = 2.0 ** -7
QR = (192, 192, 192, 192)
ORDER = (2, 1, 3, 0)
FIRST = 5 * TOK
PR = tuple(1024 - 2 * q for q in QR)
Q_MEAN = sum(QR) // NB


def kernel(h_ref, gain_ref, codes_ref, scales_ref, cot_ref, pass_ref, ig_ref, wg_ref,
           hv, cv, ct, nv, wall, cod, cq, ng, hp, part, xr, zr, zf, first, vst, gv, sv, inv, cdv, vals,
           hl_sem, l_sem, cod_sem, own_sem, h_r, ct_r, z_r, xw_r, sw_r, xr_r, zr_r, v_r, send_sem):
    sec, i, z = lax.axis_index("section"), lax.axis_index("dp"), lax.axis_index("node")
    x, y, c = i // 8, (i // 2) % 4, i % 2

    def dev(xx, yy, zz, cc, ss=None):
        return (sec if ss is None else ss, xx * 8 + yy * 2 + cc, zz)

    zp, zm, z2 = (z + 1) % 4, (z + 3) % 4, (z + 2) % 4
    yp, ym, yo = (y + 1) % 4, (y + 3) % 4, (y + 2) % 4
    d_sib, d_x = dev(x, y, z, 1 - c), dev(1 - x, y, z, c)
    d_y = {(t, k): dev(x, yy, z, c if k == 0 else 1 - c)
           for t, yy in enumerate((yp, ym, yo)) for k in range(2)}
    d_z = [None, dev(x, y, zp, c), None, dev(x, y, zm, c)]
    d_sec = dev(x, y, z, c, 1 - sec)

    def remote(src, dst, s, r, device):
        return pltpu.make_async_remote_copy(src_ref=src, dst_ref=dst, send_sem=s, recv_sem=r,
                                            device_id=device, device_id_type=MESH)

    def load_h(b):
        return pltpu.make_async_copy(h_ref.at[0, :, pl.ds(pl.multiple_of(b * BLK, BLK), BLK)], hv.at[b], hl_sem.at[0])

    def wait_bytes(ref, sem):
        pltpu.make_async_copy(ref, ref, sem).wait()

    def load_codes(kb):
        return pltpu.make_async_copy(codes_ref.at[0, :, pl.ds(kb * KB, KB)], cod.at[kb % 2], cod_sem.at[kb])

    barrier = pltpu.get_barrier_semaphore()
    for target in (d_sib, d_x, *d_y.values(), d_z[1], d_z[3], d_sec):
        pl.semaphore_signal(barrier, inc=1, device_id=target, device_id_type=MESH)

    cp_g = pltpu.make_async_copy(gain_ref, gv, l_sem.at[0])
    cp_s = pltpu.make_async_copy(scales_ref.at[0], sv, l_sem.at[1])
    cp_c = pltpu.make_async_copy(cot_ref.at[0], cv, l_sem.at[2])
    quick = 4 * c + 3 * x
    cp_q = pltpu.make_async_copy(codes_ref.at[0, pl.ds(pl.multiple_of(quick * 256, 256), 256)], cq, l_sem.at[3])
    cp_q.start()
    cp_s.start()

    @pl.loop(0, NBLK)
    def _(b):
        load_h(b).start()

    cp_c.start()
    load_codes(0).start()
    load_codes(1).start()
    cp_g.start()

    def h_copy(g, slot):
        xx = (x + 1 + g // 4) % 2
        yy = y if slot < 2 else (yp, ym, yo)[(slot - 2) % 3]
        cc = c if slot in (0, 2, 3, 4) else 1 - c
        lanes = pl.ds(pl.multiple_of(((z + ORDER[g % 4]) % 4) * 128, 128), 128)
        b = xx * 8 + yy * 2 + cc
        src, dst = hv.at[b, :, lanes], hp.at[g, pl.ds(slot * TOK, TOK)]
        if g == 0 and slot:
            col = b * BLK + ((z + ORDER[0]) % 4) * 128
            src = h_ref.at[0, :, pl.ds(pl.multiple_of(col, 128), 128)]
        if slot == 0:
            return pltpu.make_async_copy(src, dst, own_sem.at[0])
        return remote(src, dst, send_sem.at[0], h_r.at[8 if g == 7 and slot > 4 else g],
                      d_sib if slot == 1 else d_y[(slot - 2) % 3, (slot - 2) // 3])

    def h_send(g):
        for slot in (2, 3, 4, 1, 5, 6, 7):
            h_copy(g, slot).start()

    def ct_copy(k):
        def cols(slot):
            return pl.ds(slot * TOK, TOK)

        if k < 3:
            src, dst, target = ct.at[:, cols(0)], ct.at[:, cols((2, 3, 1)[k])], (d_y[0, 0], d_y[1, 0], d_sib)[k]
        elif k < 5:
            rows = pl.ds((k - 3) * (KV // 2), KV // 2)
            src, dst, target = ct.at[rows, cols((2, 3)[k - 3])], ct.at[rows, cols(4)], d_y[k - 3, 0]
        else:
            slot = (2, 3, 4)[k - 5]
            src, dst, target = ct.at[:, cols(slot)], ct.at[:, cols(slot + 3)], d_sib
        return remote(src, dst, send_sem.at[1], ct_r.at[(0, 1, 3, 2, 2, 3, 3, 3)[k]], target)

    base = c * 1024

    def row(offset):
        return pl.multiple_of(base + offset, 16)

    def z_copy(kb, k):
        if k < 4:
            start, size = row(x * (QR[kb] + PR[kb])), QR[kb]
        else:
            start, size = row(QR[kb]), PR[kb]
        half = (size + 31) // 32 * 16
        if k % 4 < 2:
            ref = wall.at[kb, z, pl.ds(start, size)]
        elif k % 4 == 2:
            ref = wall.at[kb, zm, pl.ds(start, half)]
        else:
            ref = wall.at[kb, zp, pl.ds(pl.multiple_of(start + half, 16), size - half)]
        return remote(ref, ref, send_sem.at[2], z_r.at[kb, (0, 1, 2, 2, 3, 4, 5, 5)[k]], d_z[1 if k % 2 == 0 else 3])

    shards = (zm, zp, z2)

    def x_copy(kb, k):
        ref = wall.at[kb, shards[k], pl.ds(row(x * (QR[kb] + PR[kb])), QR[kb])]
        return remote(ref, ref, send_sem.at[3], xw_r.at[kb], d_x)

    def sib_copy(kb, k):
        if k < 3:
            ref = wall.at[kb, shards[k], pl.ds(row(x * QR[kb]), PR[kb] + QR[kb])]
        else:
            ref = wall.at[kb, shards[k - 3], pl.ds(row((1 - x) * (QR[kb] + PR[kb])), QR[kb])]
        return remote(ref, ref, send_sem.at[4], sw_r.at[kb, 1 if k == 2 else 0], d_sib)

    def dequant(kb):
        load_codes(kb).wait()

        @pl.loop(1, SHARD // 256)
        def _(t):
            g = (quick + t) % (SHARD // 256)
            rows = pl.ds(pl.multiple_of(g * 256, 256), 256)
            scale = sv[pl.ds(g, 1), kb * KB:(kb + 1) * KB]
            wall[kb, z, rows, :] = (cod[kb % 2, rows, :].astype(F32) * scale).astype(BF16)

        if kb + 2 < NB:
            load_codes(kb + 2).start()

    def p_send(kb):
        z_copy(kb, 4).start()
        z_copy(kb, 5).start()

    pl.semaphore_wait(barrier, 11)
    h_send(0)
    cp_q.wait()
    cp_s.wait()
    for kb in range(NB):
        cols = slice(kb * KB, (kb + 1) * KB)
        wall[kb, z, pl.ds(pl.multiple_of(quick * 256, 256), 256), :] = (
            cq[:, cols].astype(F32) * sv[pl.ds(quick, 1), cols]).astype(BF16)
        z_copy(kb, 0).start()
        z_copy(kb, 1).start()

    def scale_cot():
        wait_bytes(hv, hl_sem.at[0])

        def squares(b, acc):
            v = hv[b].astype(F32)
            v = v * v
            return acc + (v[:, 0:128] + v[:, 128:256]) + (v[:, 256:384] + v[:, 384:512])

        acc = lax.fori_loop(0, NBLK, squares, jnp.zeros((TOK, 128), F32))
        inv[...] = jnp.broadcast_to(lax.rsqrt(jnp.sum(acc, axis=1, keepdims=True) * (1.0 / D) + 1e-05), (TOK, 128))
        cp_c.wait()
        for q in range(4):
            scaled = cv[:, q * 256:(q + 1) * 256].astype(F32) * inv[:, 0:1]
            ct[q * 256:(q + 1) * 256, 0:TOK] = jnp.transpose(scaled).astype(BF16)
        for k in range(3):
            ct_copy(k).start()
        cp_g.wait()
        for g in range(8):
            h_copy(g, 0).start()

    def ct_first(k):
        ct_copy(k).wait_recv()
        ct_copy(3 + k).start()
        ct_copy(5 + k).start()

    def ct_second():
        wait_bytes(ct.at[:, pl.ds(0, TOK)], ct_r.at[2])
        ct_copy(7).start()
        wait_bytes(ct.at[:, pl.ds(0, 4 * TOK)], ct_r.at[3])
        wait_bytes(hp.at[:, pl.ds(0, TOK)], own_sem.at[0])

    def xr_copy(g):
        return remote(part.at[g], xr.at[g], send_sem.at[5], xr_r.at[g], d_x)

    def zr_copy(m, half=0):
        up = m % 2 == 0
        if m < 2:
            rows = pl.ds(half * (KV // 2), KV // 2)
            return remote(part.at[5 + m, rows], zr.at[m, rows], send_sem.at[6], zr_r.at[m], d_z[1 if up else 3])
        rows = pl.ds((m - 2) * (KV // 2), KV // 2)
        return remote(part.at[4, rows], zf.at[m - 2], send_sem.at[6], zr_r.at[m], d_z[1 if up else 3])

    def grad_first():
        wait_bytes(hp.at[7, pl.ds(TOK, 4 * TOK)], h_r.at[7])
        for q in range(4):
            rows = slice(q * 256, (q + 1) * 256)
            first[rows, :] = jnp.dot(ct[rows, :FIRST], hp[7, :FIRST, :], preferred_element_type=F32)

    def grad(g):
        wait_bytes(hp.at[g, pl.ds(TOK, (3 if g == 7 else 7) * TOK)], h_r.at[8 if g == 7 else g])
        if g >= 4:
            xr_copy(g - 4).wait_recv()
        if g in (5, 6):
            zr_copy(g - 3).wait_recv()
        for q in range(4):
            rows = slice(q * 256, (q + 1) * 256)
            if g == 7:
                t = jnp.dot(ct[rows, FIRST:], hp[g, FIRST:, :], preferred_element_type=F32)
                t = (t + first[rows, :]) * FACTOR
            else:
                t = jnp.dot(ct[rows, :], hp[g], preferred_element_type=F32) * FACTOR
            if g >= 4:
                t = t + xr[g - 4, rows, :].astype(F32)
            if g in (5, 6) and q // 2 == g - 5:
                t = t + zf[g - 5, (q % 2) * 256:(q % 2 + 1) * 256, :].astype(F32)
            part[g, rows, :] = t.astype(BF16)
            if g in (5, 6) and q % 2:
                zr_copy(g - 5, q // 2).start()
        if g < 4:
            xr_copy(g).start()
        elif g == 4:
            zr_copy(2).start()
            zr_copy(3).start()

    d0 = pl.multiple_of(i * 512 + z * 128, 128)

    def grad_last():
        wait_bytes(zr.at[0], zr_r.at[0])
        wait_bytes(zr.at[1], zr_r.at[1])
        for q in range(4):
            rows = slice(q * 256, (q + 1) * 256)
            total = part[7, rows, :].astype(F32) + zr[0, rows, :].astype(F32) + zr[1, rows, :].astype(F32)
            total = total * gv[0:1, pl.ds(d0, 128)]
            wg_ref[0, :, rows] = jnp.transpose(total).astype(BF16)

    def w_q(kb, k):
        z_copy(kb, k).wait_recv()
        z_copy(kb, 2 + k).start()
        x_copy(kb, k).start()

    def w_p(kb, k):
        z_copy(kb, 4 + k).wait_recv()
        z_copy(kb, 6 + k).start()
        sib_copy(kb, k).start()

    def w_bq(kb):
        wait_bytes(wall.at[kb, 0, pl.ds(0, QR[kb])], z_r.at[kb, 2])
        x_copy(kb, 2).start()

    def w_bp(kb):
        wait_bytes(wall.at[kb, 0, pl.ds(0, PR[kb])], z_r.at[kb, 5])
        sib_copy(kb, 2).start()

    def w_c(kb):
        wait_bytes(wall.at[kb, pl.ds(0, 3), pl.ds(0, QR[kb])], xw_r.at[kb])
        for k in range(3):
            sib_copy(kb, 3 + k).start()

    def pass_copy(kb):
        return remote(vst.at[kb], pass_ref.at[0, :, pl.ds(kb * KB, KB)], send_sem.at[7], v_r.at[0], d_sec)

    def h_block(zz, r):
        return hv[zz * 4 + r].astype(F32)

    def gain_block(zz, r):
        return gv[0:1, pl.ds(pl.multiple_of(zz * SHARD + r * BLK, BLK), BLK)]

    def normalize():
        @pl.loop(0, NZ)
        def _(zz):
            for r in range(4):
                nv[zz, :, r * BLK:(r + 1) * BLK] = (h_block(zz, r) * inv[:, 0:1] * gain_block(zz, r)).astype(BF16)

    def grad_of(kb, zz, lo, size):
        return lax.dot_general(cv[:, kb * KB:(kb + 1) * KB], wall[kb, zz, lo:lo + size, :], (((1,), (1,)), ((), ())),
                               preferred_element_type=F32)

    def near(kb):
        wait_bytes(wall.at[kb, pl.ds(0, 2), pl.ds(0, 1024 + QR[kb] // 2)], sw_r.at[kb, 0])

    def far(kb):
        wait_bytes(wall.at[kb, 0, pl.ds(0, PR[kb] + QR[kb])], sw_r.at[kb, 1])

    def add_grad(kb, zz):
        for lo in (0, 1024):
            t = grad_of(kb, zz, lo, 1024)
            if kb == 0:
                ng[zz, :, lo:lo + 1024] = t
            else:
                ng[zz, :, lo:lo + 1024] = ng[zz, :, lo:lo + 1024] + t

    def finish(kb, vals):
        vst[kb] = vals.astype(BF16)
        pass_copy(kb).start()
        prod = vals * cv[:, kb * KB:(kb + 1) * KB].astype(F32)
        prod = prod[:, 0:128] + prod[:, 128:256]
        if kb == 0:
            cdv[...] = prod
        else:
            cdv[...] = cdv[...] + prod

    def w_d(kb):
        near(kb)
        far(kb)

        def step(zz, acc):
            add_grad(kb, zz)
            return acc + jnp.dot(nv[zz], wall[kb, zz], preferred_element_type=F32)

        finish(kb, lax.fori_loop(0, NZ, step, jnp.zeros((TOK, KB), F32)))

    def w_near():
        kb = NB - 1
        near(kb)

        def step(t, acc):
            zz = (z + t + t // 2) % NZ
            add_grad(kb, zz)
            return acc + jnp.dot(nv[zz], wall[kb, zz], preferred_element_type=F32)

        vals[...] = lax.fori_loop(0, 3, step, jnp.zeros((TOK, KB), F32))

    def w_far():
        kb = NB - 1
        far(kb)
        finish(kb, vals[...] + jnp.dot(nv[z2], wall[kb, z2], preferred_element_type=F32))
        iv = inv[:, 0:1]
        coef = iv * iv * (jnp.sum(cdv[...], axis=1, keepdims=True) * (1.0 / D))
        cdv[...] = jnp.broadcast_to(coef, (TOK, 128))

    def w_e(t):
        zz = (z + (2, 0, 1, 3)[t]) % NZ
        if t == 0:
            add_grad(NB - 1, zz)
        iv, coef = inv[:, 0:1], cdv[:, 0:1]
        for r in range(4):
            t_all = iv * gain_block(zz, r) * ng[zz, :, r * BLK:(r + 1) * BLK]
            ig_ref[0, :, pl.ds(pl.multiple_of(zz * SHARD + r * BLK, BLK), BLK)] = (
                t_all - h_block(zz, r) * coef).astype(BF16)

    scale_cot()
    dequant(0)
    p_send(0)
    dequant(1)
    h_send(1)
    w_q(0, 0)
    w_q(0, 1)
    w_q(1, 1)
    w_q(1, 0)
    w_q(2, 0)
    w_q(2, 1)
    dequant(2)
    w_q(3, 0)
    w_q(3, 1)
    w_p(0, 1)
    w_p(0, 0)
    p_send(1)
    ct_first(0)
    ct_first(1)
    h_send(2)
    w_bq(0)
    w_bq(1)
    w_bq(2)
    w_bq(3)
    normalize()
    w_c(0)
    p_send(2)
    w_bp(0)
    h_send(3)
    w_d(0)
    w_c(2)
    ct_second()
    w_c(1)
    w_c(3)
    w_p(1, 0)
    w_p(1, 1)
    grad(0)
    grad(1)
    grad(2)
    h_send(4)
    h_send(5)
    w_p(2, 0)
    w_p(2, 1)
    dequant(3)
    p_send(3)
    h_send(6)
    h_send(7)
    grad(3)
    w_bp(1)
    w_d(1)
    grad(4)
    w_bp(2)
    w_d(2)
    w_p(3, 0)
    w_p(3, 1)
    grad(5)
    w_near()
    grad(6)
    w_bp(3)
    grad_first()
    w_far()
    w_e(3)
    w_e(1)
    w_e(0)
    grad(7)
    w_e(2)
    grad_last()
    wait_bytes(pass_ref, v_r.at[0])
    wait_bytes(hp.at[:, pl.ds(0, 7 * TOK)], send_sem.at[0])
    wait_bytes(ct.at[:, pl.ds(0, 7 * TOK)], send_sem.at[1])
    wait_bytes(wall.at[:, pl.ds(0, 3), pl.ds(0, 1024 - Q_MEAN)], send_sem.at[2])
    wait_bytes(wall.at[:, pl.ds(0, 3), pl.ds(0, Q_MEAN)], send_sem.at[3])
    wait_bytes(wall.at[:, pl.ds(0, 3), pl.ds(0, 1024)], send_sem.at[4])
    wait_bytes(part.at[pl.ds(0, 4)], send_sem.at[5])
    wait_bytes(part.at[pl.ds(4, 3)], send_sem.at[6])
    wait_bytes(vst, send_sem.at[7])


def hand_over(a_in, b_in, c_in, a_out, b_out, c_out, sem):
    copies = [pltpu.make_async_copy(a_in, a_out, sem.at[0]), pltpu.make_async_copy(c_in, c_out, sem.at[1])]
    for k in range(8):
        rows = pl.ds(k * 32, 32)
        copies.append(pltpu.make_async_copy(b_in.at[0, rows], b_out.at[0, rows], sem.at[2 + k]))
    for copy in copies:
        copy.start()
    for copy in copies:
        copy.wait()


def on_device(hidden_in, norm_gain, weight_codes, block_scales, value_grad):
    dma, any_ = pltpu.SemaphoreType.DMA, pl.BlockSpec(memory_space=pl.ANY)
    v = pltpu.VMEM
    out = pl.pallas_call(
        kernel,
        out_shape=(v((1, TOK, KV), BF16), v((1, TOK, D), BF16), v((1, 128, KV), BF16)),
        in_specs=[any_] * 5,
        out_specs=[pl.BlockSpec(memory_space=v)] * 3,
        scratch_shapes=[
            v((NBLK, TOK, BLK), BF16),
            v((TOK, KV), BF16),
            v((KV, 8 * TOK), BF16),
            v((NZ, TOK, SHARD), BF16),
            v((NB, NZ, SHARD, KB), BF16),
            v((2, SHARD, KB), jnp.int32),
            v((256, KV), jnp.int32),
            v((NZ, TOK, SHARD), F32),
            v((8, 8 * TOK, 128), BF16),
            v((8, KV, 128), BF16),
            v((4, KV, 128), BF16),
            v((2, KV, 128), BF16),
            v((2, KV // 2, 128), BF16),
            v((KV, 128), F32),
            v((NB, TOK, KB), BF16),
            v((1, D), F32),
            v((8, KV), F32),
            v((TOK, 128), F32),
            v((TOK, 128), F32),
            v((TOK, KB), F32),
            dma((1,)), dma((4,)), dma((NB,)), dma((1,)), dma((9,)), dma((4,)), dma((NB, 6)), dma((NB,)), dma((NB, 2)),
            dma((4,)), dma((4,)), dma((1,)), dma((8,)),
        ],
        compiler_params=pltpu.CompilerParams(
            collective_id=0, has_side_effects=True, vmem_limit_bytes=57 * 2 ** 20),
        cost_estimate=pl.CostEstimate(flops=3 * 2 * TOK * D * KV, bytes_accessed=24 * 2 ** 20, transcendentals=TOK),
    )(hidden_in, norm_gain, weight_codes, block_scales, value_grad)
    return pl.pallas_call(
        hand_over,
        out_shape=tuple(jax.ShapeDtypeStruct(o.shape, o.dtype) for o in out),
        in_specs=[pl.BlockSpec(memory_space=v)] * 3,
        out_specs=[any_] * 3,
        scratch_shapes=[dma((10,))],
        compiler_params=pltpu.CompilerParams(vmem_limit_bytes=2 * 2 ** 20),
    )(*out)


def solution(mesh):
    return jax.shard_map(
        on_device,
        mesh=mesh,
        in_specs=(
            P("section", ("dp", "node"), None),
            P("section", None),
            P("section", "node", None),
            P("section", "node", None),
            P("section", ("dp", "node"), None),
        ),
        out_specs=(
            P("section", ("dp", "node"), None),
            P("section", ("dp", "node"), None),
            P("section", ("dp", "node"), None),
        ),
        check_vma=False,
    )
```
